32 devices in a mesh: gx: 16 (over z, x, core), gy: 2 (over y).
Axes of the slice: x: 2, y: 2, z: 4, core: 2. Of those that a mesh axis runs over, the one named last changes fastest.
Arguments:
- part_cell: int32 [557056], P(('gx', 'gy')), may hold values from 0 to 16383
- part_offset: float32 [3, 557056], P(None, ('gx', 'gy')), may hold values from 0 to 1
- part_vort: float32 [3, 557056], P(None, ('gx', 'gy')), may hold values from -6 to 6
- moving: int32 [32, 3], P(('gx', 'gy')), may hold values from 0 to 17408, as said below
Outputs:
- velocity: float32 [3, 64, 64, 128], P(None, 'gx', 'gy')
- stretching: float32 [3, 64, 64, 128], P(None, 'gx', 'gy')
The draws below stay inside these ranges and needn't reach their ends.
Inputs may be any that keep to these rules, and one draw needn't show every extreme that they name: Row r of moving belongs to the device at position r along gx+gy, with index a along gx. Its entries are p, the particles of that device's list bound for slab a - 1, q, those bound for slab a + 1, and l, the live length. The list holds the p particles for a - 1 in slots 0 to p - 1, then the q for a + 1, then the particles that stay, then unused slots from l on. p and q are at most 1024; some device has p = q = 1024 and l = 17408, and some device receives 1024 particles from each of its two neighbouring slabs.
All inputs are finite; a program needn't handle non-finite values.
Results may differ from the reference program's by a relative error of at most 0.0053.
Values sent between devices are 32-bit elements; how exact they have to be, the bound alone decides.
No kernel may reach another device: no remote copies, remote signals or barrier semaphores. Data moves between devices by JAX's collectives and lax.ppermute only.
A program may use at most 64 MiB of HBM per device.

```python
import jax
import jax.numpy as jnp
from jax import lax

CX = 4
CY = 32
NZ = 128
OUTER = 4
SWEEPS = 3
CELLS = 16384
CAP = 1024
SLOTS = 17408
NX = 64
NY = 64
PARTS_SIZE = 557056


def draw_moving(key, part):
    slab_count = NX // CX
    pencils = NY // CY
    device_count = slab_count * pencils
    subkeys = jax.random.split(key, 6)
    heavy_mask = jax.random.randint(subkeys[0], (device_count,), 0, 8) == 0
    light_next = jax.random.randint(subkeys[1], (device_count,), CAP // 8, CAP // 2 + 1)
    heavy_next = jax.random.randint(subkeys[2], (device_count,), CAP // 2, CAP + 1)
    to_next = jnp.where(heavy_mask, heavy_next, light_next)
    to_prev = jax.random.randint(subkeys[3], (device_count,), CAP // 8, CAP // 2 + 1)
    spare_slots = jax.random.randint(subkeys[4], (device_count,), 0, CAP // 2 + 1)
    chosen = jax.random.randint(subkeys[5], (), 0, device_count)
    device_ids = jnp.arange(device_count)
    target = device_ids == chosen
    partner = (chosen // pencils + 2) % slab_count * pencils + chosen % pencils
    to_next = jnp.where(target, CAP, to_next)
    to_prev = jnp.where(target | (device_ids == partner), CAP, to_prev)
    spare_slots = jnp.where(target, 0, spare_slots)
    live_len = to_prev + to_next + (SLOTS - 2 * CAP) - spare_slots
    return jnp.stack([to_prev, to_next, live_len], axis=1).astype(jnp.int32)


def plant(values, key, low, largest):
    longest = values.shape.index(max(values.shape))
    spots = []
    for shift in (0, 1):
        where = [jax.random.randint(jax.random.fold_in(key, axis), (), 0, length) for axis, length in enumerate(values.shape)]
        where[longest] = (where[longest] + shift) % values.shape[longest]
        spots.append(tuple(where))
    return values.at[spots[0]].set(low).at[spots[1]].set(largest)


def levels(key, dims, cuts, least, top_value):
    loudness = 1.0
    for position, shards_of in cuts:
        steps = jax.random.uniform(jax.random.fold_in(jax.random.fold_in(key, 6), position), (shards_of,), jnp.float32, least / len(cuts), top_value / len(cuts))
        loudness = loudness * jnp.repeat(jnp.exp(steps), dims[position] // shards_of).reshape((-1,) + (1,) * (len(dims) - 1 - position))
    return loudness


def centred(own_key, extent, spread, bound, cuts=(), held_as=jnp.bfloat16):
    result = spread * jax.random.normal(own_key, extent, jnp.float32)
    if cuts:
        result = result * levels(own_key, extent, cuts, -0.22, 0.18)
    return jnp.clip(result, -bound, bound).astype(held_as)


def setup_inputs(seed: int = 0) -> dict:
    keys = jax.random.split(jax.random.key(seed), 5)
    return {
        "part_cell": plant(jax.random.randint(keys[0], (PARTS_SIZE,), 0, CELLS), jax.random.fold_in(keys[0], 1), 0, CELLS - 1).astype(jnp.int32),
        "part_offset": jnp.clip(1.0 * jax.random.uniform(keys[1], (3, PARTS_SIZE), jnp.float32) ** levels(keys[1], (3, PARTS_SIZE), ((1, 32),), -0.2, 0.2), 0.0, 1.0),
        "part_vort": centred(keys[2], (3, PARTS_SIZE), 1.0, 6.0, ((1, 32),), jnp.float32),
        "moving": draw_moving(jax.random.fold_in(keys[4], 71), 0),
    }


def m4_weights(offset):
    remain = 1.0 - offset
    return (-0.5 * offset * remain * remain,
            1.0 - 2.5 * offset * offset + 1.5 * offset * offset * offset,
            1.0 - 2.5 * remain * remain + 1.5 * remain * remain * remain,
            -0.5 * offset * offset * remain)


def rounded(values):
    return lax.optimization_barrier(values.astype(jnp.bfloat16)).astype(jnp.float32)


def jacobi_sweep(field, source):
    centre = field[..., 1:-1, 1:-1, :]
    summed = field[..., :-2, 1:-1, :] + field[..., 2:, 1:-1, :] + field[..., 1:-1, :-2, :] + field[..., 1:-1, 2:, :]
    summed = summed + jnp.roll(centre, 1, -1) + jnp.roll(centre, -1, -1) + source
    return field.at[..., 1:-1, 1:-1, :].set(summed / 6.0)


def central(field, axis_dim):
    return (jnp.roll(field, -1, axis_dim) - jnp.roll(field, 1, axis_dim)) * 0.5


def reference(part_cell, part_offset, part_vort, moving):
    slab_count = NX // CX
    pencils = NY // CY
    device_count = slab_count * pencils
    slot_ids = jnp.arange(SLOTS, dtype=jnp.int32)[None, :]
    device_ids = jnp.arange(device_count, dtype=jnp.int32)[:, None]
    column = device_ids // pencils
    row_block = device_ids % pencils
    to_prev = moving[:, 0:1]
    to_next = moving[:, 1:2]
    live_len = moving[:, 2:3]
    slab_of = jnp.where(slot_ids < to_prev, column - 1, jnp.where(slot_ids < to_prev + to_next, column + 1, column)) % slab_count
    cell_of = part_cell.reshape(device_count, SLOTS)
    offsets = part_offset.reshape(3, device_count, SLOTS)
    strength = jnp.where((slot_ids < live_len)[None], part_vort.reshape(3, device_count, SLOTS), 0.0)
    base_x = slab_of * CX + cell_of // (CY * NZ)
    base_y = row_block * CY + (cell_of // NZ) % CY
    base_z = cell_of % NZ
    weight_x = m4_weights(offsets[0])
    weight_y = m4_weights(offsets[1])
    weight_z = m4_weights(offsets[2])
    deposit = jnp.zeros((3, NX * NY * NZ), jnp.float32)
    for tap_x in range(4):
        node_x = (base_x + (tap_x - 1)) % NX
        for tap_y in range(4):
            node_y = (base_y + (tap_y - 1)) % NY
            plane_weight = rounded(weight_x[tap_x] * weight_y[tap_y])
            for tap_z in range(4):
                node_z = (base_z + (tap_z - 1)) % NZ
                line_weight = rounded(weight_z[tap_z][None] * strength)
                contrib = plane_weight[None] * line_weight
                flat_index = ((node_x * NY + node_y) * NZ + node_z).astype(jnp.int32)
                deposit = deposit.at[:, flat_index.reshape(-1)].add(contrib.reshape(3, -1))
    omega = deposit.reshape(3, NX, NY, NZ)

    def extend(field, margin):
        index_x = ((jnp.arange(slab_count, dtype=jnp.int32)[:, None] * CX - margin + jnp.arange(CX + 2 * margin, dtype=jnp.int32)[None, :]) % NX).astype(jnp.int32)
        index_y = ((jnp.arange(pencils, dtype=jnp.int32)[:, None] * CY - margin + jnp.arange(CY + 2 * margin, dtype=jnp.int32)[None, :]) % NY).astype(jnp.int32)
        widened = field[:, index_x]
        widened = widened[:, :, :, index_y]
        return jnp.transpose(widened, (0, 1, 3, 2, 4, 5))

    source = extend(omega, 1)
    potential = jnp.zeros_like(omega)
    for outer_step in range(OUTER):
        field = extend(potential, 2)
        for repeat in range(SWEEPS):
            field = jacobi_sweep(field, source)
        interior = field[..., 2:-2, 2:-2, :]
        potential = jnp.transpose(interior, (0, 1, 3, 2, 4, 5)).reshape(3, NX, NY, NZ)
    psi_x, psi_y, psi_z = potential[0], potential[1], potential[2]
    velocity = jnp.stack([central(psi_z, 1) - central(psi_y, 2),
                          central(psi_x, 2) - central(psi_z, 0),
                          central(psi_y, 0) - central(psi_x, 1)])
    stretching = jnp.stack([omega[0] * central(velocity[comp], 0) + omega[1] * central(velocity[comp], 1) + omega[2] * central(velocity[comp], 2) for comp in range(3)])
    return velocity, stretching
```

```python
import functools

import jax
import jax.numpy as jnp
from jax import lax
from jax.experimental import pallas as pl
from jax.experimental.pallas import tpu as pltpu
from jax.sharding import PartitionSpec as P

CX = 4
CY = 32
NZ = 128
OUTER = 4
SWEEPS = 3
F32 = jnp.float32
BF16 = jnp.bfloat16
ROWS = CY + 8
PLANES = CX + 3
SPREAD = 288
QUANTITIES = 31
VMEM_BYTES = 48 * 1024 * 1024


def in_vmem(count):
    return [pl.BlockSpec(memory_space=pltpu.VMEM)] * count


def in_smem():
    return pl.BlockSpec(memory_space=pltpu.SMEM)


def params():
    return pltpu.CompilerParams(vmem_limit_bytes=VMEM_BYTES)


def across(n):
    return [(i, (i + 1) % n if i % 2 else (i - 1) % n) for i in range(n)]


def within(n):
    return [(i, i ^ 1) for i in range(n)]


def swap_x(to_within, to_across):
    n = lax.axis_size("gx")
    got_across = lax.ppermute(to_across, "gx", across(n))
    got_within = lax.ppermute(to_within, "gx", within(n))
    return got_within, got_across


def m4_weights(offset):
    remain = 1.0 - offset
    return (
        -0.5 * offset * remain * remain,
        1.0 - 2.5 * offset * offset + 1.5 * offset * offset * offset,
        1.0 - 2.5 * remain * remain + 1.5 * remain * remain * remain,
        -0.5 * offset * offset * remain,
    )


def prepare(cells, offsets, strengths, table, rows):
    weight_x, weight_y, weight_z = (m4_weights(offset) for offset in offsets)
    cell_x = cells // (CY * NZ)
    cell_y = cells // NZ % CY
    cell_z = cells % NZ
    for plane in range(PLANES):
        along = jnp.zeros_like(offsets[0])
        for tap in range(4):
            along = jnp.where(cell_x == plane - tap, weight_x[tap], along)
        table[plane, rows] = along
    for tap in range(4):
        node_y = cell_y + (tap - 1)
        if tap == 0:
            node_y = jnp.where(cell_y == 0, ROWS - 1, node_y)
        table[7 + tap, rows] = weight_y[tap]
        table[11 + tap, rows] = node_y.astype(F32)
        table[15 + tap, rows] = ((cell_z + (tap - 1)) & (NZ - 1)).astype(F32)
        for comp in range(3):
            table[19 + tap * 3 + comp, rows] = weight_z[tap] * strengths[comp]


def spread(table, first, tiles, planes, lines):
    row_ids = lax.broadcasted_iota(jnp.int32, (ROWS, 128), 0).astype(F32)
    z_ids = lax.broadcasted_iota(jnp.int32, (NZ, 128), 0).astype(F32).astype(BF16)
    for tile in range(tiles):
        lanes = slice(tile * 128, (tile + 1) * 128)

        def figure(k):
            return table[k, pl.ds(first + tile, 1)]

        along_y = jnp.zeros((ROWS, 128), F32)
        for tap in range(4):
            along_y = jnp.where(row_ids == figure(11 + tap), figure(7 + tap), along_y)
        parts = [figure(plane) * along_y for plane in range(PLANES)]
        parts.append(jnp.zeros((SPREAD - PLANES * ROWS, 128), F32))
        planes[:, lanes] = jnp.concatenate(parts, axis=0).astype(BF16)
        masks = [z_ids == figure(15 + tap).astype(BF16) for tap in range(4)]
        for comp in range(3):
            line = jnp.zeros((NZ, 128), BF16)
            for tap in range(4):
                line = jnp.where(masks[tap], figure(19 + tap * 3 + comp).astype(BF16), line)
            lines[comp * NZ : (comp + 1) * NZ, lanes] = line


def product(planes, lines):
    return lax.dot_general(
        planes[...], lines[...], (((1,), (1,)), ((), ())), preferred_element_type=F32
    )


def staying_kernel(
    limits, cell_hbm, offset_hbm, vort_hbm, total, cells, offsets, vorts, dense, table,
    planes_a, lines_a, planes_b, lines_b, sems, *, tiles_per_chunk,
):
    first_stay = limits[0] + limits[1]
    live_len = limits[2]
    tiles = cells.shape[0]
    copies = [
        pltpu.make_async_copy(offset_hbm, offsets, sems.at[0]),
        pltpu.make_async_copy(vort_hbm, vorts, sems.at[1]),
        pltpu.make_async_copy(cell_hbm, cells, sems.at[2]),
    ]
    for copy in copies:
        copy.start()
    total[...] = jnp.zeros_like(total)
    for copy in copies:
        copy.wait()
    for tile in range(tiles):
        lanes = slice(tile * 128, (tile + 1) * 128)
        for dim in range(3):
            dense[dim, tile : tile + 1] = offsets[dim : dim + 1, lanes]
            dense[3 + dim, tile : tile + 1] = vorts[dim : dim + 1, lanes]

    def one_group(group, carry):
        rows = pl.ds(pl.multiple_of(group * 8, 8), 8)
        slot = (
            group * 1024
            + lax.broadcasted_iota(jnp.int32, (8, 128), 0) * 128
            + lax.broadcasted_iota(jnp.int32, (8, 128), 1)
        )
        keep = (slot >= first_stay) & (slot < live_len)
        prepare(
            cells[rows],
            [dense[dim, rows] for dim in range(3)],
            [jnp.where(keep, dense[3 + dim, rows], 0.0) for dim in range(3)],
            table,
            rows,
        )
        return carry

    lax.fori_loop(0, tiles // 8, one_group, 0)
    chunks = tiles // tiles_per_chunk
    spread(table, 0, tiles_per_chunk, planes_a, lines_a)

    def two_chunks(pair, carry):
        spread(table, (2 * pair + 1) * tiles_per_chunk, tiles_per_chunk, planes_b, lines_b)
        total[...] += product(planes_a, lines_a)
        spread(table, (2 * pair + 2) * tiles_per_chunk, tiles_per_chunk, planes_a, lines_a)
        total[...] += product(planes_b, lines_b)
        return carry

    lax.fori_loop(0, (chunks - 1) // 2, two_chunks, 0)
    if chunks % 2 == 0:
        spread(table, (chunks - 1) * tiles_per_chunk, tiles_per_chunk, planes_b, lines_b)
        total[...] += product(planes_a, lines_a)
        total[...] += product(planes_b, lines_b)
    else:
        total[...] += product(planes_a, lines_a)


def deposit_staying(part_cell, part_offset, part_vort, limits):
    slots = part_cell.shape[0]
    tiles = slots // 128
    per_chunk = 17
    chunk = per_chunk * 128
    return pl.pallas_call(
        functools.partial(staying_kernel, tiles_per_chunk=per_chunk),
        in_specs=[in_smem()] + [pl.BlockSpec(memory_space=pl.ANY)] * 3,
        out_specs=in_vmem(1)[0],
        out_shape=jax.ShapeDtypeStruct((SPREAD, 3 * NZ), F32),
        scratch_shapes=[
            pltpu.VMEM((tiles, 128), jnp.int32),
            pltpu.VMEM((3, slots), F32),
            pltpu.VMEM((3, slots), F32),
            pltpu.VMEM((6, tiles, 128), F32),
            pltpu.VMEM((QUANTITIES, tiles, 128), F32),
        ]
        + [pltpu.VMEM((SPREAD, chunk), BF16), pltpu.VMEM((3 * NZ, chunk), BF16)] * 2
        + [pltpu.SemaphoreType.DMA((3,))],
        compiler_params=params(),
        cost_estimate=pl.CostEstimate(
            flops=2 * SPREAD * 3 * NZ * slots, bytes_accessed=28 * slots, transcendentals=0
        ),
    )(limits, part_cell.reshape(tiles, 128), part_offset, part_vort)


def arrived_kernel(side, total, got_within, got_across, deposits, to_within, to_across, dense, table, planes, lines):
    tiles = got_within.shape[1] // 128
    for which, got in enumerate((got_within, got_across)):
        for tile in range(tiles):
            lanes = slice(tile * 128, (tile + 1) * 128)
            place = which * tiles + tile
            for k in range(7):
                dense[k, place : place + 1] = got[k : k + 1, lanes]
    for group in range(2 * tiles // 8):
        rows = slice(group * 8, (group + 1) * 8)
        prepare(
            dense[6, rows].astype(jnp.int32),
            [dense[dim, rows] for dim in range(3)],
            [dense[3 + dim, rows] for dim in range(3)],
            table,
            rows,
        )
    spread(table, 0, 2 * tiles, planes, lines)
    whole = total[...] + product(planes, lines)
    for comp in range(3):
        for plane in range(PLANES):
            deposits[comp, plane] = whole[
                plane * ROWS : (plane + 1) * ROWS, comp * NZ : (comp + 1) * NZ
            ]
    first_within = jnp.where(side[0] == 0, CX, 0)
    first_across = jnp.where(side[0] == 0, 0, CX)
    to_within[...] = deposits[:, pl.ds(first_within, 3)]
    to_across[...] = deposits[:, pl.ds(first_across, 3)]


def deposit_arrived(side, total, got_within, got_across):
    received = got_within.shape[1]
    edge = jax.ShapeDtypeStruct((3, 3, ROWS, NZ), F32)
    tiles = 2 * received // 128
    return pl.pallas_call(
        arrived_kernel,
        in_specs=[in_smem()] + in_vmem(3),
        out_specs=tuple(in_vmem(3)),
        out_shape=(jax.ShapeDtypeStruct((3, PLANES, ROWS, NZ), F32), edge, edge),
        scratch_shapes=[
            pltpu.VMEM((7, tiles, 128), F32),
            pltpu.VMEM((QUANTITIES, tiles, 128), F32),
            pltpu.VMEM((SPREAD, 2 * received), BF16),
            pltpu.VMEM((3 * NZ, 2 * received), BF16),
        ],
        compiler_params=params(),
    )(side, total, got_within, got_across)


def leaving(part_cell, part_offset, part_vort, limits):
    capacity = part_cell.shape[0] // 17
    room = 2 * capacity
    packed = jnp.concatenate(
        [part_offset[:, :room], part_vort[:, :room], part_cell[:room].astype(F32)[None]], axis=0
    )
    ids = jnp.arange(capacity, dtype=jnp.int32)[None]
    to_prev = jnp.where(ids < limits[0], packed[:, :capacity], 0.0)
    shifted = lax.dynamic_slice_in_dim(packed, limits[0], capacity, 1)
    to_next = jnp.where(ids < limits[1], shifted, 0.0)
    return to_prev, to_next


def edge_rows(low, high):
    ids = lax.broadcasted_iota(jnp.int32, (8, NZ), 0)
    return jnp.where(ids < 4, low, high)


def edged_plane(mine, other):
    return jnp.concatenate([mine, edge_rows(other[:8], other[-8:])], axis=0)


def roll_rows(value, shift):
    return pltpu.roll(value, shift % value.shape[0], 0)


def roll_z(value, shift):
    return pltpu.roll(value, shift % NZ, 1)


def relax(fields, sources):
    ids = lax.broadcasted_iota(jnp.int32, (ROWS, NZ), 0)
    frozen = (ids > CY) & (ids < ROWS - 1)
    for sweep in range(SWEEPS):
        fresh = list(fields)
        last = sweep == SWEEPS - 1
        for x in range(2 if last else 1, CX + (2 if last else 3)):
            centre = fields[x]
            summed = fields[x - 1] + fields[x + 1] + roll_rows(centre, 1) + roll_rows(centre, -1)
            summed = summed + roll_z(centre, 1) + roll_z(centre, -1) + sources[x - 1]
            fresh[x] = jnp.where(frozen, centre, summed * (1.0 / 6.0))
        fields = fresh
    return fields[2 : CX + 2]


def hand_out(side, potential, to_within, to_across):
    first_within = jnp.where(side[0] == 0, CX - 2, 0)
    first_across = jnp.where(side[0] == 0, 0, CX - 2)
    rows = to_within.shape[2]
    if rows == 2 * CY:
        to_within[...] = potential[:, pl.ds(first_within, 2)]
        to_across[...] = potential[:, pl.ds(first_across, 2)]
    else:
        for first, out in ((first_within, to_within), (first_across, to_across)):
            out[:, :, : CY + 8] = potential[:, pl.ds(first, 2), : CY + 8]
            out[:, :, CY + 8 :] = potential[:, pl.ds(first, 2), 2 * CY - 8 :]


def first_kernel(side, mine, other, omega, potential, to_within, to_across):
    ids = lax.broadcasted_iota(jnp.int32, (8, NZ), 0)

    def folded(main, edges):
        low = main[:8] + jnp.where(ids < 2, edges, 0.0)
        high = main[CY - 8 : CY] + jnp.where(ids == 7, edges, 0.0)
        return jnp.concatenate([low, main[8 : CY - 8], high], axis=0)

    def one_component(comp, carry):
        sources = ([], [])
        for x in range(CX + 2):
            a = mine[comp, x]
            b = other[comp, x]
            omega_a = folded(a[:CY], b[CY:])
            omega_b = folded(b[:CY], a[CY:])
            omega[comp, x, :CY] = omega_a
            omega[comp, x, CY:] = omega_b
            sources[0].append(edged_plane(omega_a, omega_b))
            sources[1].append(edged_plane(omega_b, omega_a))
        for block in range(2):
            fields = [jnp.zeros((ROWS, NZ), F32)] * (CX + 4)
            fields = relax(fields, sources[block])
            for x in range(CX):
                potential[comp, x, block * CY : (block + 1) * CY] = fields[x][:CY]
        return carry

    lax.fori_loop(0, 3, one_component, 0)
    hand_out(side, potential, to_within, to_across)


def ring_planes(side, got_within, got_across, comp):
    even = side[0] == 0

    def both(got, x):
        value = got[comp, x]
        if value.shape[0] == 2 * CY:
            return value[:CY], value[CY:]
        high = value[CY + 8 :]
        return value[:CY], jnp.concatenate([value[CY : CY + 8], high, high, high], axis=0)

    def chosen(pick, x):
        inner, outer = both(got_within, x), both(got_across, x)
        return tuple(jnp.where(pick, a, b) for a, b in zip(inner, outer))

    below = [chosen(jnp.logical_not(even), x) for x in range(2)]
    above = [chosen(even, x) for x in range(2)]
    return below, above


def gathered(side, potential, got_within, got_across, comp):
    below, above = ring_planes(side, got_within, got_across, comp)
    middle = [(potential[comp, x, :CY], potential[comp, x, CY:]) for x in range(CX)]
    return below + middle + above


def next_kernel(side, omega, before, got_within, got_across, potential, to_within, to_across):
    def one_component(comp, carry):
        pairs = gathered(side, before, got_within, got_across, comp)
        charge = [(omega[comp, x, :CY], omega[comp, x, CY:]) for x in range(CX + 2)]
        for block in range(2):
            fields = [edged_plane(pair[block], pair[1 - block]) for pair in pairs]
            sources = [edged_plane(pair[block], pair[1 - block]) for pair in charge]
            fields = relax(fields, sources)
            for x in range(CX):
                potential[comp, x, block * CY : (block + 1) * CY] = fields[x][:CY]
        return carry

    lax.fori_loop(0, 3, one_component, 0)
    hand_out(side, potential, to_within, to_across)


def last_kernel(side, omega, potential, got_within, got_across, velocity, stretching):
    psi = []
    for comp in range(3):
        pairs = gathered(side, potential, got_within, got_across, comp)
        psi.append([edged_plane(a, b) for a, b in pairs])

    def slope_x(planes, x):
        return (planes[x + 1] - planes[x - 1]) * 0.5

    def slope_y(plane):
        return (roll_rows(plane, -1) - roll_rows(plane, 1)) * 0.5

    def slope_z(plane):
        return (roll_z(plane, -1) - roll_z(plane, 1)) * 0.5

    speeds = ([None], [None], [None])
    for x in range(1, CX + 3):
        speeds[0].append(slope_y(psi[2][x]) - slope_z(psi[1][x]))
        speeds[1].append(slope_z(psi[0][x]) - slope_x(psi[2], x))
        speeds[2].append(slope_x(psi[1], x) - slope_y(psi[0][x]))
    for comp in range(3):
        for x in range(CX):
            centre = speeds[comp][x + 2]
            velocity[comp, x] = centre[:CY]
            stretching[comp, x] = (
                omega[0, x + 1, :CY] * slope_x(speeds[comp], x + 2)[:CY]
                + omega[1, x + 1, :CY] * slope_y(centre)[:CY]
                + omega[2, x + 1, :CY] * slope_z(centre)[:CY]
            )


def edge_shape(rows):
    return jax.ShapeDtypeStruct((3, 2, rows, NZ), F32)


def two_block_solve(side, deposits, to_within, to_across):
    got_within, got_across = swap_x(to_within, to_across)
    even = side[0] == 0
    from_prev = jnp.where(even, got_across, got_within)
    from_next = jnp.where(even, got_within, got_across)[:, :2]
    none = ((0, 0), (0, 0))
    mine = (
        deposits[:, : CX + 2]
        + jnp.pad(from_prev, ((0, 0), (0, CX - 1)) + none)
        + jnp.pad(from_next, ((0, 0), (CX, 0)) + none)
    )
    other = lax.ppermute(mine, "gy", [(0, 1), (1, 0)])
    slab = jax.ShapeDtypeStruct((3, CX, 2 * CY, NZ), F32)
    omega, potential, to_within, to_across = pl.pallas_call(
        first_kernel,
        in_specs=[in_smem()] + in_vmem(2),
        out_specs=tuple(in_vmem(4)),
        out_shape=(
            jax.ShapeDtypeStruct((3, CX + 2, 2 * CY, NZ), F32),
            slab,
            edge_shape(2 * CY),
            edge_shape(2 * CY),
        ),
        compiler_params=params(),
    )(side, mine, other)
    for _ in range(1, OUTER):
        got_within, got_across = swap_x(to_within, to_across)
        potential, to_within, to_across = pl.pallas_call(
            next_kernel,
            in_specs=[in_smem()] + in_vmem(4),
            out_specs=tuple(in_vmem(3)),
            out_shape=(slab, edge_shape(CY + 16), edge_shape(CY + 16)),
            compiler_params=params(),
        )(side, omega, potential, got_within, got_across)
    got_within, got_across = swap_x(to_within, to_across)
    block = jax.ShapeDtypeStruct((3, CX, CY, NZ), F32)
    return pl.pallas_call(
        last_kernel,
        in_specs=[in_smem()] + in_vmem(4),
        out_specs=tuple(in_vmem(2)),
        out_shape=(block, block),
        compiler_params=params(),
    )(side, omega, potential, got_within, got_across)


def padded(value, sides, width):
    for axis, dim in sides:
        devices, length = (lax.axis_size(axis), value.shape[dim])
        up = [(i, (i + 1) % devices) for i in range(devices)]
        down = [(j, i) for i, j in up]
        last = lax.slice_in_dim(value, length - width, length, axis=dim)
        leading = lax.slice_in_dim(value, 0, width, axis=dim)
        before = lax.ppermute(last, axis, up)
        after = lax.ppermute(leading, axis, down)
        value = jnp.concatenate([before, value, after], axis=dim)
    return value


def jacobi_sweep(field, source):
    centre = field[..., 1:-1, 1:-1, :]
    summed = (
        field[..., :-2, 1:-1, :]
        + field[..., 2:, 1:-1, :]
        + field[..., 1:-1, :-2, :]
        + field[..., 1:-1, 2:, :]
    )
    summed = summed + jnp.roll(centre, 1, -1) + jnp.roll(centre, -1, -1) + source
    return field.at[..., 1:-1, 1:-1, :].set(summed / 6.0)


def slope_x(field):
    return (field[2:, 1:-1] - field[:-2, 1:-1]) * 0.5


def slope_y(field):
    return (field[1:-1, 2:] - field[1:-1, :-2]) * 0.5


def slope_z(field):
    centre = field[1:-1, 1:-1]
    return (jnp.roll(centre, -1, -1) - jnp.roll(centre, 1, -1)) * 0.5


def fold_ghosts(extended, axis_dim, extent):
    centre = lax.slice_in_dim(extended, 4, extent + 4, axis=axis_dim)
    low_rim = lax.slice_in_dim(extended, 0, 2, axis=axis_dim)
    high_rim = lax.slice_in_dim(extended, extent + 6, extent + 8, axis=axis_dim)
    pad_low = [(0, 0)] * extended.ndim
    pad_high = [(0, 0)] * extended.ndim
    pad_low[axis_dim] = (0, extent - 2)
    pad_high[axis_dim] = (extent - 2, 0)
    return centre + jnp.pad(low_rim, pad_low) + jnp.pad(high_rim, pad_high)


def general_solve(deposits):
    sides = (("gx", 1), ("gy", 2))
    rows = jnp.concatenate(
        [jnp.zeros_like(deposits[:, :, :1]), deposits[:, :, ROWS - 1 :], deposits[:, :, : CY + 2]],
        axis=2,
    )
    full = jnp.pad(rows, ((0, 0), (1, 0), (0, 0), (0, 0)))
    omega = fold_ghosts(fold_ghosts(padded(full, sides, 2), 1, CX), 2, CY)
    source = padded(omega, sides, 2)[:, 1:-1, 1:-1]
    potential = jnp.zeros_like(omega)
    for _ in range(OUTER):
        field = padded(potential, sides, 2)
        for _ in range(SWEEPS):
            field = jacobi_sweep(field, source)
        potential = field[:, 2:-2, 2:-2]
    wide = padded(potential, sides, 2)
    edged_velocity = jnp.stack(
        [
            slope_y(wide[2]) - slope_z(wide[1]),
            slope_z(wide[0]) - slope_x(wide[2]),
            slope_x(wide[1]) - slope_y(wide[0]),
        ]
    )
    stretching = jnp.stack(
        [
            omega[0] * slope_x(edged_velocity[comp])
            + omega[1] * slope_y(edged_velocity[comp])
            + omega[2] * slope_z(edged_velocity[comp])
            for comp in range(3)
        ]
    )
    return edged_velocity[:, 1:-1, 1:-1], stretching


def per_device(part_cell, part_offset, part_vort, moving):
    limits = moving[0]
    side = (lax.axis_index("gx") % 2).astype(jnp.int32)[None]
    even = side[0] == 0
    to_prev, to_next = leaving(part_cell, part_offset, part_vort, limits)
    got_within, got_across = swap_x(
        jnp.where(even, to_next, to_prev), jnp.where(even, to_prev, to_next)
    )
    total = deposit_staying(part_cell, part_offset, part_vort, limits)
    deposits, to_within, to_across = deposit_arrived(side, total, got_within, got_across)
    if lax.axis_size("gy") == 2:
        return two_block_solve(side, deposits, to_within, to_across)
    return general_solve(deposits)


def solution(mesh):
    return jax.shard_map(
        per_device,
        mesh=mesh,
        in_specs=(
            P(("gx", "gy")),
            P(None, ("gx", "gy")),
            P(None, ("gx", "gy")),
            P(("gx", "gy"), None),
        ),
        out_specs=(P(None, "gx", "gy", None), P(None, "gx", "gy", None)),
        check_vma=False,
    )
```

```python
import functools

import jax
import jax.numpy as jnp
from jax import lax
from jax.experimental import pallas as pl
from jax.experimental.pallas import tpu as pltpu
from jax.sharding import PartitionSpec as P

CX = 4
CY = 32
NZ = 128
OUTER = 4
SWEEPS = 3
F32 = jnp.float32
BF16 = jnp.bfloat16
ROWS = CY + 8
PLANES = CX + 3
SPREAD = 288
QUANTITIES = 25
VMEM_BYTES = 48 * 1024 * 1024


def in_vmem(count):
    return [pl.BlockSpec(memory_space=pltpu.VMEM)] * count


def in_smem():
    return pl.BlockSpec(memory_space=pltpu.SMEM)


def params():
    return pltpu.CompilerParams(vmem_limit_bytes=VMEM_BYTES)


def is_even():
    return lax.axis_index("gx") % 2 == 0


def across(n):
    return [(i, (i + 1) % n if i % 2 else (i - 1) % n) for i in range(n)]


def within(n):
    return [(i, i ^ 1) for i in range(n)]


def swap_x(to_within, to_across):
    n = lax.axis_size("gx")
    got_across = lax.ppermute(to_across, "gx", across(n))
    got_within = lax.ppermute(to_within, "gx", within(n))
    return got_within, got_across


def m4_weights(offset):
    remain = 1.0 - offset
    return (
        -0.5 * offset * remain * remain,
        1.0 - 2.5 * offset * offset + 1.5 * offset * offset * offset,
        1.0 - 2.5 * remain * remain + 1.5 * remain * remain * remain,
        -0.5 * offset * offset * remain,
    )


def prepare(cells, offsets, strengths, table, rows):
    weight_x, weight_y, weight_z = (m4_weights(offset) for offset in offsets)
    cell_x = cells // (CY * NZ)
    cell_y = cells // NZ % CY
    cell_z = cells % NZ
    for plane in range(PLANES):
        along = jnp.zeros_like(offsets[0])
        for tap in range(4):
            along = jnp.where(cell_x == plane - tap, weight_x[tap], along)
        table[plane, rows] = along
    table[11, rows] = (cell_y - 1).astype(F32)
    table[12, rows] = ((cell_z - 1) & (NZ - 1)).astype(F32)
    for tap in range(4):
        table[7 + tap, rows] = weight_y[tap]
        for comp in range(3):
            table[13 + tap * 3 + comp, rows] = weight_z[tap] * strengths[comp]


def spread(table, first, tiles, planes, lines):
    ids = lax.broadcasted_iota(jnp.int32, (8, 128), 0)
    zero = jnp.zeros((8, 128), F32)
    half = lax.broadcasted_iota(jnp.int32, (16, 128), 0) // 8
    none = jnp.zeros((16, 128), BF16)
    for tile in range(tiles):
        lanes = slice(tile * 128, (tile + 1) * 128)

        def figure(k):
            return table[k, pl.ds(first + tile, 1)]

        first_row = figure(11).astype(jnp.int32)
        tap_of = (ids - first_row) & 7
        row = first_row + tap_of
        row_tile = jnp.where(row < 0, CY // 8, row >> 3)
        taps = zero
        for tap in range(4):
            taps = jnp.where(tap_of == tap, figure(7 + tap), taps)
        along_y = [jnp.where(row_tile == k, taps, 0.0) for k in range(ROWS // 8)]
        parts = [figure(plane) * piece for plane in range(PLANES) for piece in along_y]
        parts += [zero] * ((SPREAD - PLANES * ROWS) // 8)
        planes[:, lanes] = jnp.concatenate(parts, axis=0).astype(BF16)

        first_z = figure(12).astype(jnp.int32)
        tap_of = (ids - first_z) & 7
        z_tile = (((first_z + tap_of) & (NZ - 1)) >> 3).astype(F32)
        where_tap = [tap_of == tap for tap in range(4)]
        pair = (jnp.concatenate([z_tile, z_tile], axis=0) - half.astype(F32)).astype(BF16)
        doubled = []
        for comp in range(3):
            taps = zero
            for tap in range(4):
                taps = jnp.where(where_tap[tap], figure(13 + tap * 3 + comp), taps)
            doubled.append(jnp.concatenate([taps, taps], axis=0).astype(BF16))
        for k in range(NZ // 16):
            here = pair == jnp.asarray(2.0 * k, BF16)
            for comp in range(3):
                start = comp * NZ + 16 * k
                lines[start : start + 16, lanes] = jnp.where(here, doubled[comp], none)


def product(planes, lines):
    return lax.dot_general(
        planes[...], lines[...], (((1,), (1,)), ((), ())), preferred_element_type=F32
    )


def leaving_kernel(
    moving, cell_hbm, offset_hbm, vort_hbm, cells, offsets, vorts, to_within, to_across, packed, sems, *, capacity
):
    copies = [
        pltpu.make_async_copy(offset_hbm, offsets, sems.at[0]),
        pltpu.make_async_copy(vort_hbm, vorts, sems.at[1]),
        pltpu.make_async_copy(cell_hbm, cells, sems.at[2]),
    ]
    for copy in copies:
        copy.start()
    even = is_even()
    prev_count = moving[0, 0]
    next_count = moving[0, 1]
    for copy in copies:
        copy.wait()
    room = 2 * capacity
    packed[0:3] = offsets[:, :room]
    packed[3:6] = vorts[:, :room]
    for tile in range(room // 128):
        packed[6:7, tile * 128 : (tile + 1) * 128] = cells[tile : tile + 1].astype(F32)
    packed[7:8] = jnp.zeros((1, room), F32)
    ids = lax.broadcasted_iota(jnp.int32, (8, capacity), 1)
    listed = packed[...]
    shifted = pltpu.roll(listed, (room - prev_count) % room, 1)
    for_prev = jnp.where(ids < prev_count, listed[:, :capacity], 0.0)
    for_next = jnp.where(ids < next_count, shifted[:, :capacity], 0.0)
    to_within[...] = jnp.where(even, for_next, for_prev)
    to_across[...] = jnp.where(even, for_prev, for_next)


def pack_leaving(part_cell, part_offset, part_vort, moving):
    slots = part_cell.shape[0]
    capacity = slots // 17
    tiles = slots // 128
    message = jax.ShapeDtypeStruct((8, capacity), F32)
    return pl.pallas_call(
        functools.partial(leaving_kernel, capacity=capacity),
        in_specs=[in_smem()] + [pl.BlockSpec(memory_space=pltpu.HBM)] * 3,
        out_specs=tuple(in_vmem(5)),
        out_shape=(
            jax.ShapeDtypeStruct((tiles, 128), jnp.int32),
            jax.ShapeDtypeStruct((3, slots), F32),
            jax.ShapeDtypeStruct((3, slots), F32),
            message,
            message,
        ),
        scratch_shapes=[pltpu.VMEM((8, 2 * capacity), F32), pltpu.SemaphoreType.DMA((3,))],
        compiler_params=params(),
    )(moving, part_cell.reshape(tiles, 128), part_offset, part_vort)


def staying_kernel(
    moving, cells, offsets, vorts, total, dense, table, planes_a, lines_a, planes_b, lines_b, *, tiles_per_chunk
):
    first_stay = moving[0, 0] + moving[0, 1]
    live_len = moving[0, 2]
    tiles = cells.shape[0]
    total[...] = jnp.zeros_like(total)
    for tile in range(tiles):
        lanes = slice(tile * 128, (tile + 1) * 128)
        for dim in range(3):
            dense[dim, tile : tile + 1] = offsets[dim : dim + 1, lanes]
            dense[3 + dim, tile : tile + 1] = vorts[dim : dim + 1, lanes]

    def one_group(group, carry):
        rows = pl.ds(pl.multiple_of(group * 8, 8), 8)
        slot = (
            group * 1024
            + lax.broadcasted_iota(jnp.int32, (8, 128), 0) * 128
            + lax.broadcasted_iota(jnp.int32, (8, 128), 1)
        )
        keep = (slot >= first_stay) & (slot < live_len)
        prepare(
            cells[rows],
            [dense[dim, rows] for dim in range(3)],
            [jnp.where(keep, dense[3 + dim, rows], 0.0) for dim in range(3)],
            table,
            rows,
        )
        return carry

    lax.fori_loop(0, tiles // 8, one_group, 0)
    chunks = tiles // tiles_per_chunk
    spread(table, 0, tiles_per_chunk, planes_a, lines_a)

    def two_chunks(pair, carry):
        spread(table, (2 * pair + 1) * tiles_per_chunk, tiles_per_chunk, planes_b, lines_b)
        total[...] += product(planes_a, lines_a)
        spread(table, (2 * pair + 2) * tiles_per_chunk, tiles_per_chunk, planes_a, lines_a)
        total[...] += product(planes_b, lines_b)
        return carry

    lax.fori_loop(0, (chunks - 1) // 2, two_chunks, 0)
    if chunks % 2 == 0:
        spread(table, (chunks - 1) * tiles_per_chunk, tiles_per_chunk, planes_b, lines_b)
        total[...] += product(planes_a, lines_a)
        total[...] += product(planes_b, lines_b)
    else:
        total[...] += product(planes_a, lines_a)


def deposit_staying(cells, offsets, vorts, moving):
    tiles = cells.shape[0]
    slots = tiles * 128
    per_chunk = 17
    chunk = per_chunk * 128
    return pl.pallas_call(
        functools.partial(staying_kernel, tiles_per_chunk=per_chunk),
        in_specs=[in_smem()] + in_vmem(3),
        out_specs=in_vmem(1)[0],
        out_shape=jax.ShapeDtypeStruct((SPREAD, 3 * NZ), F32),
        scratch_shapes=[
            pltpu.VMEM((6, tiles, 128), F32),
            pltpu.VMEM((QUANTITIES, tiles, 128), F32),
        ]
        + [pltpu.VMEM((SPREAD, chunk), BF16), pltpu.VMEM((3 * NZ, chunk), BF16)] * 2,
        compiler_params=params(),
        cost_estimate=pl.CostEstimate(
            flops=2 * SPREAD * 3 * NZ * slots, bytes_accessed=28 * slots, transcendentals=0
        ),
    )(moving, cells, offsets, vorts)


def arrived_kernel(total, got_within, got_across, deposits, to_within, to_across, dense, table, planes, lines):
    tiles = got_within.shape[1] // 128
    for which, got in enumerate((got_within, got_across)):
        for tile in range(tiles):
            lanes = slice(tile * 128, (tile + 1) * 128)
            place = which * tiles + tile
            for k in range(7):
                dense[k, place : place + 1] = got[k : k + 1, lanes]
    for group in range(2 * tiles // 8):
        rows = slice(group * 8, (group + 1) * 8)
        prepare(
            dense[6, rows].astype(jnp.int32),
            [dense[dim, rows] for dim in range(3)],
            [dense[3 + dim, rows] for dim in range(3)],
            table,
            rows,
        )
    spread(table, 0, 2 * tiles, planes, lines)
    whole = total[...] + product(planes, lines)
    for comp in range(3):
        for plane in range(PLANES):
            deposits[comp, plane] = whole[
                plane * ROWS : (plane + 1) * ROWS, comp * NZ : (comp + 1) * NZ
            ]
    even = is_even()
    first_within = jnp.where(even, CX, 0)
    first_across = jnp.where(even, 0, CX)
    to_within[...] = deposits[:, pl.ds(first_within, 3)]
    to_across[...] = deposits[:, pl.ds(first_across, 3)]


def deposit_arrived(total, got_within, got_across):
    received = got_within.shape[1]
    edge = jax.ShapeDtypeStruct((3, 3, ROWS, NZ), F32)
    tiles = 2 * received // 128
    return pl.pallas_call(
        arrived_kernel,
        in_specs=in_vmem(3),
        out_specs=tuple(in_vmem(3)),
        out_shape=(jax.ShapeDtypeStruct((3, PLANES, ROWS, NZ), F32), edge, edge),
        scratch_shapes=[
            pltpu.VMEM((7, tiles, 128), F32),
            pltpu.VMEM((QUANTITIES, tiles, 128), F32),
            pltpu.VMEM((SPREAD, 2 * received), BF16),
            pltpu.VMEM((3 * NZ, 2 * received), BF16),
        ],
        compiler_params=params(),
    )(total, got_within, got_across)


def edge_rows(low, high):
    ids = lax.broadcasted_iota(jnp.int32, (8, NZ), 0)
    return jnp.where(ids < 4, low, high)


def edged_plane(mine, other):
    return jnp.concatenate([mine, edge_rows(other[:8], other[-8:])], axis=0)


def roll_rows(value, shift):
    return pltpu.roll(value, shift % value.shape[0], 0)


def roll_z(value, shift):
    return pltpu.roll(value, shift % NZ, 1)


def relax(fields, sources):
    ids = lax.broadcasted_iota(jnp.int32, (ROWS, NZ), 0)
    frozen = (ids > CY) & (ids < ROWS - 1)
    for sweep in range(SWEEPS):
        fresh = list(fields)
        last = sweep == SWEEPS - 1
        for x in range(2 if last else 1, CX + (2 if last else 3)):
            centre = fields[x]
            summed = fields[x - 1] + fields[x + 1] + roll_rows(centre, 1) + roll_rows(centre, -1)
            summed = summed + roll_z(centre, 1) + roll_z(centre, -1) + sources[x - 1]
            fresh[x] = jnp.where(frozen, centre, summed * (1.0 / 6.0))
        fields = fresh
    return fields[2 : CX + 2]


def pack_rows(a, b, rows):
    ids = lax.broadcasted_iota(jnp.int32, (8, NZ), 0)
    first, last = b[:8], b[CY - 8 :]
    if rows == CY + 8:
        return jnp.concatenate([a, jnp.where(ids < 4, first, last)], axis=0)
    if rows == CY + 16:
        return jnp.concatenate([a, first, last], axis=0)
    middle = jnp.where(ids < 4, b[8:16], b[CY - 16 : CY - 8])
    return jnp.concatenate([a, first, middle, last], axis=0)


def unpack_rows(packed):
    a, rest = packed[:CY], packed[CY:]
    first, last = rest[:8], rest[rest.shape[0] - 8 :]
    middle = rest[8:16] if rest.shape[0] == 24 else last
    return a, jnp.concatenate([first, middle, middle, last], axis=0)


def hand_out(potential, to_within, to_across):
    even = is_even()
    rows = to_within.shape[2]
    for comp in range(3):
        for x in range(2):
            low, high = (
                pack_rows(potential[comp, at, :CY], potential[comp, at, CY:], rows)
                for at in (x, CX - 2 + x)
            )
            to_within[comp, x] = jnp.where(even, high, low)
            to_across[comp, x] = jnp.where(even, low, high)


def fold_kernel(deposits, got_within, got_across, mine, message):
    even = is_even()
    ids = lax.broadcasted_iota(jnp.int32, (8, NZ), 0)
    for comp in range(3):
        for x in range(CX + 2):
            value = deposits[comp, x]
            if x < 3:
                value = value + jnp.where(even, got_across[comp, x], got_within[comp, x])
            if x >= CX:
                value = value + jnp.where(even, got_within[comp, x - CX], got_across[comp, x - CX])
            mine[comp, x] = value
            edges = value[CY:]
            third = jnp.where(ids < 2, edges, jnp.where(ids == 2, roll_rows(edges, 3), value[16:24]))
            message[comp, x] = jnp.concatenate([value[:16], third, value[24:CY]], axis=0)


def first_kernel(mine, other, omega, potential, to_within, to_across):
    ids = lax.broadcasted_iota(jnp.int32, (8, NZ), 0)

    def folded(main, edges):
        low = main[:8] + jnp.where(ids < 2, edges, 0.0)
        high = main[CY - 8 : CY] + jnp.where(ids == 7, edges, 0.0)
        return jnp.concatenate([low, main[8 : CY - 8], high], axis=0)

    def one_component(comp, carry):
        sources = ([], [])
        for x in range(CX + 2):
            a = mine[comp, x]
            b = other[comp, x]
            third = b[16:24]
            b_edges = jnp.where(ids < 2, third, roll_rows(third, 5))
            omega_a = folded(a[:CY], b_edges)
            omega_b = folded(b, a[CY:])
            omega[comp, x, :CY] = omega_a
            omega[comp, x, CY:] = omega_b
            sources[0].append(edged_plane(omega_a, omega_b))
            sources[1].append(edged_plane(omega_b, omega_a))
        for block in range(2):
            fields = [jnp.zeros((ROWS, NZ), F32)] * (CX + 4)
            fields = relax(fields, sources[block])
            for x in range(CX):
                potential[comp, x, block * CY : (block + 1) * CY] = fields[x][:CY]
        return carry

    lax.fori_loop(0, 3, one_component, 0)
    hand_out(potential, to_within, to_across)


def gathered(potential, got_within, got_across, comp):
    even = is_even()

    def chosen(pick, x):
        return unpack_rows(jnp.where(pick, got_within[comp, x], got_across[comp, x]))

    below = [chosen(jnp.logical_not(even), x) for x in range(2)]
    above = [chosen(even, x) for x in range(2)]
    middle = [(potential[comp, x, :CY], potential[comp, x, CY:]) for x in range(CX)]
    return below + middle + above


def next_kernel(omega, before, got_within, got_across, potential, to_within, to_across):
    def one_component(comp, carry):
        pairs = gathered(before, got_within, got_across, comp)
        charge = [(omega[comp, x, :CY], omega[comp, x, CY:]) for x in range(CX + 2)]
        for block in range(2):
            fields = [edged_plane(pair[block], pair[1 - block]) for pair in pairs]
            sources = [edged_plane(pair[block], pair[1 - block]) for pair in charge]
            fields = relax(fields, sources)
            for x in range(CX):
                potential[comp, x, block * CY : (block + 1) * CY] = fields[x][:CY]
        return carry

    lax.fori_loop(0, 3, one_component, 0)
    hand_out(potential, to_within, to_across)


def last_kernel(omega, potential, got_within, got_across, velocity, stretching):
    psi = []
    for comp in range(3):
        pairs = gathered(potential, got_within, got_across, comp)
        psi.append([edged_plane(a, b) for a, b in pairs])

    def slope_x(planes, x):
        return (planes[x + 1] - planes[x - 1]) * 0.5

    def slope_y(plane):
        return (roll_rows(plane, -1) - roll_rows(plane, 1)) * 0.5

    def slope_z(plane):
        return (roll_z(plane, -1) - roll_z(plane, 1)) * 0.5

    speeds = ([None], [None], [None])
    for x in range(1, CX + 3):
        speeds[0].append(slope_y(psi[2][x]) - slope_z(psi[1][x]))
        speeds[1].append(slope_z(psi[0][x]) - slope_x(psi[2], x))
        speeds[2].append(slope_x(psi[1], x) - slope_y(psi[0][x]))
    for comp in range(3):
        for x in range(CX):
            centre = speeds[comp][x + 2]
            velocity[comp, x] = centre[:CY]
            stretching[comp, x] = (
                omega[0, x + 1, :CY] * slope_x(speeds[comp], x + 2)[:CY]
                + omega[1, x + 1, :CY] * slope_y(centre)[:CY]
                + omega[2, x + 1, :CY] * slope_z(centre)[:CY]
            )


def array(*shape):
    return jax.ShapeDtypeStruct(shape, F32)


def on_vmem(kernel, outs, *args):
    return pl.pallas_call(
        kernel,
        in_specs=in_vmem(len(args)),
        out_specs=tuple(in_vmem(len(outs))),
        out_shape=outs,
        compiler_params=params(),
    )(*args)


def two_block_solve(deposits, to_within, to_across):
    planes = CX + 2
    mine, message = on_vmem(
        fold_kernel,
        (array(3, planes, ROWS, NZ), array(3, planes, CY, NZ)),
        deposits,
        *swap_x(to_within, to_across),
    )
    other = lax.ppermute(message, "gy", [(0, 1), (1, 0)])
    slab = array(3, CX, 2 * CY, NZ)
    depths = [CY + 24, CY + 16, CY + 16, CY + 8]
    edge = array(3, 2, depths[0], NZ)
    omega, potential, to_within, to_across = on_vmem(
        first_kernel, (array(3, planes, 2 * CY, NZ), slab, edge, edge), mine, other
    )
    for depth in depths[1:]:
        edge = array(3, 2, depth, NZ)
        potential, to_within, to_across = on_vmem(
            next_kernel, (slab, edge, edge), omega, potential, *swap_x(to_within, to_across)
        )
    block = array(3, CX, CY, NZ)
    return on_vmem(
        last_kernel, (block, block), omega, potential, *swap_x(to_within, to_across)
    )


def padded(value, sides, width):
    for axis, dim in sides:
        devices, length = (lax.axis_size(axis), value.shape[dim])
        up = [(i, (i + 1) % devices) for i in range(devices)]
        down = [(j, i) for i, j in up]
        last = lax.slice_in_dim(value, length - width, length, axis=dim)
        leading = lax.slice_in_dim(value, 0, width, axis=dim)
        before = lax.ppermute(last, axis, up)
        after = lax.ppermute(leading, axis, down)
        value = jnp.concatenate([before, value, after], axis=dim)
    return value


def jacobi_sweep(field, source):
    centre = field[..., 1:-1, 1:-1, :]
    summed = (
        field[..., :-2, 1:-1, :]
        + field[..., 2:, 1:-1, :]
        + field[..., 1:-1, :-2, :]
        + field[..., 1:-1, 2:, :]
    )
    summed = summed + jnp.roll(centre, 1, -1) + jnp.roll(centre, -1, -1) + source
    return field.at[..., 1:-1, 1:-1, :].set(summed / 6.0)


def slope_x(field):
    return (field[2:, 1:-1] - field[:-2, 1:-1]) * 0.5


def slope_y(field):
    return (field[1:-1, 2:] - field[1:-1, :-2]) * 0.5


def slope_z(field):
    centre = field[1:-1, 1:-1]
    return (jnp.roll(centre, -1, -1) - jnp.roll(centre, 1, -1)) * 0.5


def fold_ghosts(extended, axis_dim, extent):
    centre = lax.slice_in_dim(extended, 4, extent + 4, axis=axis_dim)
    low_rim = lax.slice_in_dim(extended, 0, 2, axis=axis_dim)
    high_rim = lax.slice_in_dim(extended, extent + 6, extent + 8, axis=axis_dim)
    pad_low = [(0, 0)] * extended.ndim
    pad_high = [(0, 0)] * extended.ndim
    pad_low[axis_dim] = (0, extent - 2)
    pad_high[axis_dim] = (extent - 2, 0)
    return centre + jnp.pad(low_rim, pad_low) + jnp.pad(high_rim, pad_high)


def general_solve(deposits):
    sides = (("gx", 1), ("gy", 2))
    rows = jnp.concatenate(
        [jnp.zeros_like(deposits[:, :, :1]), deposits[:, :, ROWS - 1 :], deposits[:, :, : CY + 2]],
        axis=2,
    )
    full = jnp.pad(rows, ((0, 0), (1, 0), (0, 0), (0, 0)))
    omega = fold_ghosts(fold_ghosts(padded(full, sides, 2), 1, CX), 2, CY)
    source = padded(omega, sides, 2)[:, 1:-1, 1:-1]
    potential = jnp.zeros_like(omega)
    for _ in range(OUTER):
        field = padded(potential, sides, 2)
        for _ in range(SWEEPS):
            field = jacobi_sweep(field, source)
        potential = field[:, 2:-2, 2:-2]
    wide = padded(potential, sides, 2)
    edged_velocity = jnp.stack(
        [
            slope_y(wide[2]) - slope_z(wide[1]),
            slope_z(wide[0]) - slope_x(wide[2]),
            slope_x(wide[1]) - slope_y(wide[0]),
        ]
    )
    stretching = jnp.stack(
        [
            omega[0] * slope_x(edged_velocity[comp])
            + omega[1] * slope_y(edged_velocity[comp])
            + omega[2] * slope_z(edged_velocity[comp])
            for comp in range(3)
        ]
    )
    return edged_velocity[:, 1:-1, 1:-1], stretching


def per_device(part_cell, part_offset, part_vort, moving):
    cells, offsets, vorts, to_within, to_across = pack_leaving(
        part_cell, part_offset, part_vort, moving
    )
    got_within, got_across = swap_x(to_within, to_across)
    total = deposit_staying(cells, offsets, vorts, moving)
    deposits, to_within, to_across = deposit_arrived(total, got_within, got_across)
    if lax.axis_size("gy") == 2:
        return two_block_solve(deposits, to_within, to_across)
    return general_solve(deposits)


def solution(mesh):
    return jax.shard_map(
        per_device,
        mesh=mesh,
        in_specs=(
            P(("gx", "gy")),
            P(None, ("gx", "gy")),
            P(None, ("gx", "gy")),
            P(("gx", "gy"), None),
        ),
        out_specs=(P(None, "gx", "gy", None), P(None, "gx", "gy", None)),
        check_vma=False,
    )
```

```python
import functools

import jax
import jax.numpy as jnp
from jax import lax
from jax.experimental import pallas as pl
from jax.experimental.pallas import tpu as pltpu
from jax.sharding import PartitionSpec as P

CX = 4
CY = 32
NZ = 128
OUTER = 4
SWEEPS = 3
F32 = jnp.float32
BF16 = jnp.bfloat16
ROWS = CY + 8
PLANES = CX + 3
SPREAD = 288
QUANTITIES = 25
VMEM_BYTES = 48 * 1024 * 1024
ALL_VMEM_BYTES = 63 * 1024 * 1024
STAY_VMEM_BYTES = 63 * 1024 * 1024


def in_vmem(count):
    return [pl.BlockSpec(memory_space=pltpu.VMEM)] * count


def in_smem():
    return pl.BlockSpec(memory_space=pltpu.SMEM)


def params(vmem_bytes=VMEM_BYTES):
    return pltpu.CompilerParams(vmem_limit_bytes=vmem_bytes)


def is_even():
    return lax.axis_index("gx") % 2 == 0


def across(n):
    return [(i, (i + 1) % n if i % 2 else (i - 1) % n) for i in range(n)]


def within(n):
    return [(i, i ^ 1) for i in range(n)]


def swap_x(to_within, to_across):
    n = lax.axis_size("gx")
    got_across = lax.ppermute(to_across, "gx", across(n))
    got_within = lax.ppermute(to_within, "gx", within(n))
    return got_within, got_across


def m4_weights(offset):
    remain = 1.0 - offset
    return (
        -0.5 * offset * remain * remain,
        1.0 - 2.5 * offset * offset + 1.5 * offset * offset * offset,
        1.0 - 2.5 * remain * remain + 1.5 * remain * remain * remain,
        -0.5 * offset * offset * remain,
    )


def prepare(cells, offsets, strengths, table, rows):
    weight_x, weight_y, weight_z = (m4_weights(offset) for offset in offsets)
    cell_x = cells // (CY * NZ)
    cell_y = cells // NZ % CY
    cell_z = cells % NZ
    for plane in range(PLANES):
        along = jnp.zeros_like(offsets[0])
        for tap in range(4):
            along = jnp.where(cell_x == plane - tap, weight_x[tap], along)
        table[plane, rows] = along
    table[11, rows] = (cell_y - 1).astype(F32)
    table[12, rows] = ((cell_z - 1) & (NZ - 1)).astype(F32)
    for tap in range(4):
        table[7 + tap, rows] = weight_y[tap]
        for comp in range(3):
            table[13 + tap * 3 + comp, rows] = weight_z[tap] * strengths[comp]


def spread(table, first, tiles, planes, lines):
    ids = lax.broadcasted_iota(jnp.int32, (8, 128), 0)
    zero = jnp.zeros((8, 128), F32)
    half = lax.broadcasted_iota(jnp.int32, (16, 128), 0) // 8
    none = jnp.zeros((16, 128), BF16)
    for tile in range(tiles):
        lanes = slice(tile * 128, (tile + 1) * 128)

        def figure(k):
            return table[k, pl.ds(first + tile, 1)]

        first_row = figure(11).astype(jnp.int32)
        tap_of = (ids - first_row) & 7
        row = first_row + tap_of
        row_tile = jnp.where(row < 0, CY // 8, row >> 3)
        taps = zero
        for tap in range(4):
            taps = jnp.where(tap_of == tap, figure(7 + tap), taps)
        along_y = [jnp.where(row_tile == k, taps, 0.0) for k in range(ROWS // 8)]
        parts = [figure(plane) * piece for plane in range(PLANES) for piece in along_y]
        parts += [zero] * ((SPREAD - PLANES * ROWS) // 8)
        planes[:, lanes] = jnp.concatenate(parts, axis=0).astype(BF16)

        first_z = figure(12).astype(jnp.int32)
        tap_of = (ids - first_z) & 7
        z_tile = (((first_z + tap_of) & (NZ - 1)) >> 3).astype(F32)
        where_tap = [tap_of == tap for tap in range(4)]
        pair = (jnp.concatenate([z_tile, z_tile], axis=0) - half.astype(F32)).astype(BF16)
        doubled = []
        for comp in range(3):
            taps = zero
            for tap in range(4):
                taps = jnp.where(where_tap[tap], figure(13 + tap * 3 + comp), taps)
            doubled.append(jnp.concatenate([taps, taps], axis=0).astype(BF16))
        for k in range(NZ // 16):
            here = pair == jnp.asarray(2.0 * k, BF16)
            for comp in range(3):
                start = comp * NZ + 16 * k
                lines[start : start + 16, lanes] = jnp.where(here, doubled[comp], none)


def product(planes, lines):
    return lax.dot_general(
        planes[...], lines[...], (((1,), (1,)), ((), ())), preferred_element_type=F32
    )


def leaving_kernel(
    moving, cell_hbm, offset_hbm, vort_hbm, to_within, to_across, cells, offsets, vorts, packed, sems, *, capacity
):
    room = 2 * capacity
    copies = [
        pltpu.make_async_copy(offset_hbm.at[:, pl.ds(0, room)], offsets, sems.at[0]),
        pltpu.make_async_copy(vort_hbm.at[:, pl.ds(0, room)], vorts, sems.at[1]),
        pltpu.make_async_copy(cell_hbm.at[pl.ds(0, room // 128)], cells, sems.at[2]),
    ]
    for copy in copies:
        copy.start()
    even = is_even()
    prev_count = moving[0, 0]
    next_count = moving[0, 1]
    for copy in copies:
        copy.wait()
    packed[0:3] = offsets[...]
    packed[3:6] = vorts[...]
    for tile in range(room // 128):
        packed[6:7, tile * 128 : (tile + 1) * 128] = cells[tile : tile + 1].astype(F32)
    packed[7:8] = jnp.zeros((1, room), F32)
    ids = lax.broadcasted_iota(jnp.int32, (8, capacity), 1)
    listed = packed[...]
    shifted = pltpu.roll(listed, (room - prev_count) % room, 1)
    for_prev = jnp.where(ids < prev_count, listed[:, :capacity], 0.0)
    for_next = jnp.where(ids < next_count, shifted[:, :capacity], 0.0)
    to_within[...] = jnp.where(even, for_next, for_prev)
    to_across[...] = jnp.where(even, for_prev, for_next)


def particle_specs():
    return [in_smem()] + [pl.BlockSpec(memory_space=pl.ANY)] * 3


def pack_leaving(moving, cells, part_offset, part_vort):
    slots = part_offset.shape[1]
    capacity = slots // 17
    room = 2 * capacity
    message = jax.ShapeDtypeStruct((8, capacity), F32)
    return pl.pallas_call(
        functools.partial(leaving_kernel, capacity=capacity),
        in_specs=particle_specs(),
        out_specs=tuple(in_vmem(2)),
        out_shape=(message, message),
        scratch_shapes=[
            pltpu.VMEM((room // 128, 128), jnp.int32),
            pltpu.VMEM((3, room), F32),
            pltpu.VMEM((3, room), F32),
            pltpu.VMEM((8, room), F32),
            pltpu.SemaphoreType.DMA((3,)),
        ],
        compiler_params=params(ALL_VMEM_BYTES),
    )(moving, cells, part_offset, part_vort)


def staying_kernel(
    moving, cell_hbm, offset_hbm, vort_hbm, total, cells, offsets, vorts, dense, table,
    planes_a, lines_a, planes_b, lines_b, sems, *, tiles_per_chunk,
):
    copies = [
        pltpu.make_async_copy(offset_hbm, offsets, sems.at[0]),
        pltpu.make_async_copy(vort_hbm, vorts, sems.at[1]),
        pltpu.make_async_copy(cell_hbm, cells, sems.at[2]),
    ]
    for copy in copies:
        copy.start()
    first_stay = moving[0, 0] + moving[0, 1]
    live_len = moving[0, 2]
    tiles = cells.shape[0]
    total[...] = jnp.zeros_like(total)
    for copy in copies:
        copy.wait()
    for tile in range(tiles):
        lanes = slice(tile * 128, (tile + 1) * 128)
        for dim in range(3):
            dense[dim, tile : tile + 1] = offsets[dim : dim + 1, lanes]
            dense[3 + dim, tile : tile + 1] = vorts[dim : dim + 1, lanes]

    def one_group(group, carry):
        rows = pl.ds(pl.multiple_of(group * 8, 8), 8)
        slot = (
            group * 1024
            + lax.broadcasted_iota(jnp.int32, (8, 128), 0) * 128
            + lax.broadcasted_iota(jnp.int32, (8, 128), 1)
        )
        keep = (slot >= first_stay) & (slot < live_len)
        prepare(
            cells[rows],
            [dense[dim, rows] for dim in range(3)],
            [jnp.where(keep, dense[3 + dim, rows], 0.0) for dim in range(3)],
            table,
            rows,
        )
        return carry

    lax.fori_loop(0, tiles // 8, one_group, 0)
    chunks = tiles // tiles_per_chunk
    spread(table, 0, tiles_per_chunk, planes_a, lines_a)

    def two_chunks(pair, carry):
        spread(table, (2 * pair + 1) * tiles_per_chunk, tiles_per_chunk, planes_b, lines_b)
        total[...] += product(planes_a, lines_a)
        spread(table, (2 * pair + 2) * tiles_per_chunk, tiles_per_chunk, planes_a, lines_a)
        total[...] += product(planes_b, lines_b)
        return carry

    lax.fori_loop(0, (chunks - 1) // 2, two_chunks, 0)
    if chunks % 2 == 0:
        spread(table, (chunks - 1) * tiles_per_chunk, tiles_per_chunk, planes_b, lines_b)
        total[...] += product(planes_a, lines_a)
        total[...] += product(planes_b, lines_b)
    else:
        total[...] += product(planes_a, lines_a)


def deposit_staying(moving, cells, part_offset, part_vort):
    tiles = cells.shape[0]
    slots = tiles * 128
    per_chunk = 17
    chunk = per_chunk * 128
    return pl.pallas_call(
        functools.partial(staying_kernel, tiles_per_chunk=per_chunk),
        in_specs=particle_specs(),
        out_specs=in_vmem(1)[0],
        out_shape=jax.ShapeDtypeStruct((SPREAD, 3 * NZ), F32),
        scratch_shapes=[
            pltpu.VMEM((tiles, 128), jnp.int32),
            pltpu.VMEM((3, slots), F32),
            pltpu.VMEM((3, slots), F32),
            pltpu.VMEM((6, tiles, 128), F32),
            pltpu.VMEM((QUANTITIES, tiles, 128), F32),
        ]
        + [pltpu.VMEM((SPREAD, chunk), BF16), pltpu.VMEM((3 * NZ, chunk), BF16)] * 2
        + [pltpu.SemaphoreType.DMA((3,))],
        compiler_params=params(STAY_VMEM_BYTES),
        cost_estimate=pl.CostEstimate(
            flops=2 * SPREAD * 3 * NZ * slots, bytes_accessed=28 * slots, transcendentals=0
        ),
    )(moving, cells, part_offset, part_vort)


def arrived_kernel(total, got_within, got_across, deposits, to_within, to_across, dense, table, planes, lines):
    tiles = got_within.shape[1] // 128
    for which, got in enumerate((got_within, got_across)):
        for tile in range(tiles):
            lanes = slice(tile * 128, (tile + 1) * 128)
            place = which * tiles + tile
            for k in range(7):
                dense[k, place : place + 1] = got[k : k + 1, lanes]
    for group in range(2 * tiles // 8):
        rows = slice(group * 8, (group + 1) * 8)
        prepare(
            dense[6, rows].astype(jnp.int32),
            [dense[dim, rows] for dim in range(3)],
            [dense[3 + dim, rows] for dim in range(3)],
            table,
            rows,
        )
    spread(table, 0, 2 * tiles, planes, lines)
    whole = total[...] + product(planes, lines)
    for comp in range(3):
        for plane in range(PLANES):
            deposits[comp, plane] = whole[
                plane * ROWS : (plane + 1) * ROWS, comp * NZ : (comp + 1) * NZ
            ]
    even = is_even()
    first_within = jnp.where(even, CX, 0)
    first_across = jnp.where(even, 0, CX)
    to_within[...] = deposits[:, pl.ds(first_within, 3)]
    to_across[...] = deposits[:, pl.ds(first_across, 3)]


def deposit_arrived(total, got_within, got_across):
    received = got_within.shape[1]
    edge = jax.ShapeDtypeStruct((3, 3, ROWS, NZ), F32)
    tiles = 2 * received // 128
    return pl.pallas_call(
        arrived_kernel,
        in_specs=in_vmem(3),
        out_specs=tuple(in_vmem(3)),
        out_shape=(jax.ShapeDtypeStruct((3, PLANES, ROWS, NZ), F32), edge, edge),
        scratch_shapes=[
            pltpu.VMEM((7, tiles, 128), F32),
            pltpu.VMEM((QUANTITIES, tiles, 128), F32),
            pltpu.VMEM((SPREAD, 2 * received), BF16),
            pltpu.VMEM((3 * NZ, 2 * received), BF16),
        ],
        compiler_params=params(),
    )(total, got_within, got_across)


def edge_rows(low, high):
    ids = lax.broadcasted_iota(jnp.int32, (8, NZ), 0)
    return jnp.where(ids < 4, low, high)


def edged_plane(mine, other):
    return jnp.concatenate([mine, edge_rows(other[:8], other[-8:])], axis=0)


def roll_rows(value, shift):
    return pltpu.roll(value, shift % value.shape[0], 0)


def roll_z(value, shift):
    return pltpu.roll(value, shift % NZ, 1)


def relax(fields, sources):
    ids = lax.broadcasted_iota(jnp.int32, (ROWS, NZ), 0)
    frozen = (ids > CY) & (ids < ROWS - 1)
    for sweep in range(SWEEPS):
        fresh = list(fields)
        last = sweep == SWEEPS - 1
        for x in range(2 if last else 1, CX + (2 if last else 3)):
            centre = fields[x]
            summed = fields[x - 1] + fields[x + 1] + roll_rows(centre, 1) + roll_rows(centre, -1)
            summed = summed + roll_z(centre, 1) + roll_z(centre, -1) + sources[x - 1]
            fresh[x] = jnp.where(frozen, centre, summed * (1.0 / 6.0))
        fields = fresh
    return fields[2 : CX + 2]


def pack_rows(a, b, rows):
    ids = lax.broadcasted_iota(jnp.int32, (8, NZ), 0)
    first, last = b[:8], b[CY - 8 :]
    if rows == CY + 8:
        return jnp.concatenate([a, jnp.where(ids < 4, first, last)], axis=0)
    if rows == CY + 16:
        return jnp.concatenate([a, first, last], axis=0)
    middle = jnp.where(ids < 4, b[8:16], b[CY - 16 : CY - 8])
    return jnp.concatenate([a, first, middle, last], axis=0)


def unpack_rows(packed):
    a, rest = packed[:CY], packed[CY:]
    first, last = rest[:8], rest[rest.shape[0] - 8 :]
    middle = rest[8:16] if rest.shape[0] == 24 else last
    return a, jnp.concatenate([first, middle, middle, last], axis=0)


def hand_out(potential, to_within, to_across):
    even = is_even()
    rows = to_within.shape[2]
    for comp in range(3):
        for x in range(2):
            low, high = (
                pack_rows(potential[comp, at, :CY], potential[comp, at, CY:], rows)
                for at in (x, CX - 2 + x)
            )
            to_within[comp, x] = jnp.where(even, high, low)
            to_across[comp, x] = jnp.where(even, low, high)


def fold_kernel(deposits, got_within, got_across, mine, message):
    even = is_even()
    ids = lax.broadcasted_iota(jnp.int32, (8, NZ), 0)
    for comp in range(3):
        for x in range(CX + 2):
            value = deposits[comp, x]
            if x < 3:
                value = value + jnp.where(even, got_across[comp, x], got_within[comp, x])
            if x >= CX:
                value = value + jnp.where(even, got_within[comp, x - CX], got_across[comp, x - CX])
            mine[comp, x] = value
            edges = value[CY:]
            third = jnp.where(ids < 2, edges, jnp.where(ids == 2, roll_rows(edges, 3), value[16:24]))
            message[comp, x] = jnp.concatenate([value[:16], third, value[24:CY]], axis=0)


def first_kernel(mine, other, omega, potential, to_within, to_across):
    ids = lax.broadcasted_iota(jnp.int32, (8, NZ), 0)

    def folded(main, edges):
        low = main[:8] + jnp.where(ids < 2, edges, 0.0)
        high = main[CY - 8 : CY] + jnp.where(ids == 7, edges, 0.0)
        return jnp.concatenate([low, main[8 : CY - 8], high], axis=0)

    def one_component(comp, carry):
        sources = ([], [])
        for x in range(CX + 2):
            a = mine[comp, x]
            b = other[comp, x]
            third = b[16:24]
            b_edges = jnp.where(ids < 2, third, roll_rows(third, 5))
            omega_a = folded(a[:CY], b_edges)
            omega_b = folded(b, a[CY:])
            omega[comp, x, :CY] = omega_a
            omega[comp, x, CY:] = omega_b
            sources[0].append(edged_plane(omega_a, omega_b))
            sources[1].append(edged_plane(omega_b, omega_a))
        for block in range(2):
            fields = [jnp.zeros((ROWS, NZ), F32)] * (CX + 4)
            fields = relax(fields, sources[block])
            for x in range(CX):
                potential[comp, x, block * CY : (block + 1) * CY] = fields[x][:CY]
        return carry

    lax.fori_loop(0, 3, one_component, 0)
    hand_out(potential, to_within, to_across)


def gathered(potential, got_within, got_across, comp):
    even = is_even()

    def chosen(pick, x):
        return unpack_rows(jnp.where(pick, got_within[comp, x], got_across[comp, x]))

    below = [chosen(jnp.logical_not(even), x) for x in range(2)]
    above = [chosen(even, x) for x in range(2)]
    middle = [(potential[comp, x, :CY], potential[comp, x, CY:]) for x in range(CX)]
    return below + middle + above


def next_kernel(omega, before, got_within, got_across, potential, to_within, to_across):
    def one_component(comp, carry):
        pairs = gathered(before, got_within, got_across, comp)
        charge = [(omega[comp, x, :CY], omega[comp, x, CY:]) for x in range(CX + 2)]
        for block in range(2):
            fields = [edged_plane(pair[block], pair[1 - block]) for pair in pairs]
            sources = [edged_plane(pair[block], pair[1 - block]) for pair in charge]
            fields = relax(fields, sources)
            for x in range(CX):
                potential[comp, x, block * CY : (block + 1) * CY] = fields[x][:CY]
        return carry

    lax.fori_loop(0, 3, one_component, 0)
    hand_out(potential, to_within, to_across)


def last_kernel(omega, potential, got_within, got_across, velocity, stretching):
    psi = []
    for comp in range(3):
        pairs = gathered(potential, got_within, got_across, comp)
        psi.append([edged_plane(a, b) for a, b in pairs])

    def slope_x(planes, x):
        return (planes[x + 1] - planes[x - 1]) * 0.5

    def slope_y(plane):
        return (roll_rows(plane, -1) - roll_rows(plane, 1)) * 0.5

    def slope_z(plane):
        return (roll_z(plane, -1) - roll_z(plane, 1)) * 0.5

    speeds = ([None], [None], [None])
    for x in range(1, CX + 3):
        speeds[0].append(slope_y(psi[2][x]) - slope_z(psi[1][x]))
        speeds[1].append(slope_z(psi[0][x]) - slope_x(psi[2], x))
        speeds[2].append(slope_x(psi[1], x) - slope_y(psi[0][x]))
    for comp in range(3):
        for x in range(CX):
            centre = speeds[comp][x + 2]
            velocity[comp, x] = centre[:CY]
            stretching[comp, x] = (
                omega[0, x + 1, :CY] * slope_x(speeds[comp], x + 2)[:CY]
                + omega[1, x + 1, :CY] * slope_y(centre)[:CY]
                + omega[2, x + 1, :CY] * slope_z(centre)[:CY]
            )


def array(*shape):
    return jax.ShapeDtypeStruct(shape, F32)


def on_vmem(kernel, outs, *args):
    return pl.pallas_call(
        kernel,
        in_specs=in_vmem(len(args)),
        out_specs=tuple(in_vmem(len(outs))),
        out_shape=outs,
        compiler_params=params(),
    )(*args)


def two_block_solve(deposits, to_within, to_across):
    planes = CX + 2
    mine, message = on_vmem(
        fold_kernel,
        (array(3, planes, ROWS, NZ), array(3, planes, CY, NZ)),
        deposits,
        *swap_x(to_within, to_across),
    )
    other = lax.ppermute(message, "gy", [(0, 1), (1, 0)])
    slab = array(3, CX, 2 * CY, NZ)
    depths = [CY + 24, CY + 16, CY + 16, CY + 8]
    edge = array(3, 2, depths[0], NZ)
    omega, potential, to_within, to_across = on_vmem(
        first_kernel, (array(3, planes, 2 * CY, NZ), slab, edge, edge), mine, other
    )
    for depth in depths[1:]:
        edge = array(3, 2, depth, NZ)
        potential, to_within, to_across = on_vmem(
            next_kernel, (slab, edge, edge), omega, potential, *swap_x(to_within, to_across)
        )
    block = array(3, CX, CY, NZ)
    return on_vmem(
        last_kernel, (block, block), omega, potential, *swap_x(to_within, to_across)
    )


def padded(value, sides, width):
    for axis, dim in sides:
        devices, length = (lax.axis_size(axis), value.shape[dim])
        up = [(i, (i + 1) % devices) for i in range(devices)]
        down = [(j, i) for i, j in up]
        last = lax.slice_in_dim(value, length - width, length, axis=dim)
        leading = lax.slice_in_dim(value, 0, width, axis=dim)
        before = lax.ppermute(last, axis, up)
        after = lax.ppermute(leading, axis, down)
        value = jnp.concatenate([before, value, after], axis=dim)
    return value


def jacobi_sweep(field, source):
    centre = field[..., 1:-1, 1:-1, :]
    summed = (
        field[..., :-2, 1:-1, :]
        + field[..., 2:, 1:-1, :]
        + field[..., 1:-1, :-2, :]
        + field[..., 1:-1, 2:, :]
    )
    summed = summed + jnp.roll(centre, 1, -1) + jnp.roll(centre, -1, -1) + source
    return field.at[..., 1:-1, 1:-1, :].set(summed / 6.0)


def slope_x(field):
    return (field[2:, 1:-1] - field[:-2, 1:-1]) * 0.5


def slope_y(field):
    return (field[1:-1, 2:] - field[1:-1, :-2]) * 0.5


def slope_z(field):
    centre = field[1:-1, 1:-1]
    return (jnp.roll(centre, -1, -1) - jnp.roll(centre, 1, -1)) * 0.5


def fold_ghosts(extended, axis_dim, extent):
    centre = lax.slice_in_dim(extended, 4, extent + 4, axis=axis_dim)
    low_rim = lax.slice_in_dim(extended, 0, 2, axis=axis_dim)
    high_rim = lax.slice_in_dim(extended, extent + 6, extent + 8, axis=axis_dim)
    pad_low = [(0, 0)] * extended.ndim
    pad_high = [(0, 0)] * extended.ndim
    pad_low[axis_dim] = (0, extent - 2)
    pad_high[axis_dim] = (extent - 2, 0)
    return centre + jnp.pad(low_rim, pad_low) + jnp.pad(high_rim, pad_high)


def general_solve(deposits):
    sides = (("gx", 1), ("gy", 2))
    rows = jnp.concatenate(
        [jnp.zeros_like(deposits[:, :, :1]), deposits[:, :, ROWS - 1 :], deposits[:, :, : CY + 2]],
        axis=2,
    )
    full = jnp.pad(rows, ((0, 0), (1, 0), (0, 0), (0, 0)))
    omega = fold_ghosts(fold_ghosts(padded(full, sides, 2), 1, CX), 2, CY)
    source = padded(omega, sides, 2)[:, 1:-1, 1:-1]
    potential = jnp.zeros_like(omega)
    for _ in range(OUTER):
        field = padded(potential, sides, 2)
        for _ in range(SWEEPS):
            field = jacobi_sweep(field, source)
        potential = field[:, 2:-2, 2:-2]
    wide = padded(potential, sides, 2)
    edged_velocity = jnp.stack(
        [
            slope_y(wide[2]) - slope_z(wide[1]),
            slope_z(wide[0]) - slope_x(wide[2]),
            slope_x(wide[1]) - slope_y(wide[0]),
        ]
    )
    stretching = jnp.stack(
        [
            omega[0] * slope_x(edged_velocity[comp])
            + omega[1] * slope_y(edged_velocity[comp])
            + omega[2] * slope_z(edged_velocity[comp])
            for comp in range(3)
        ]
    )
    return edged_velocity[:, 1:-1, 1:-1], stretching


def per_device(part_cell, part_offset, part_vort, moving):
    particles = (moving, part_cell.reshape(-1, 128), part_offset, part_vort)
    got_within, got_across = swap_x(*pack_leaving(*particles))
    total = deposit_staying(*particles)
    deposits, to_within, to_across = deposit_arrived(total, got_within, got_across)
    if lax.axis_size("gy") == 2:
        return two_block_solve(deposits, to_within, to_across)
    return general_solve(deposits)


def solution(mesh):
    return jax.shard_map(
        per_device,
        mesh=mesh,
        in_specs=(
            P(("gx", "gy")),
            P(None, ("gx", "gy")),
            P(None, ("gx", "gy")),
            P(("gx", "gy"), None),
        ),
        out_specs=(P(None, "gx", "gy", None), P(None, "gx", "gy", None)),
        check_vma=False,
    )
```

```python
import functools

import jax
import jax.numpy as jnp
from jax import lax
from jax.experimental import pallas as pl
from jax.experimental.pallas import tpu as pltpu
from jax.sharding import PartitionSpec as P

CX = 4
CY = 32
NZ = 128
OUTER = 4
SWEEPS = 3
F32 = jnp.float32
BF16 = jnp.bfloat16
ROWS = CY + 8
PLANES = CX + 3
SPREAD = 288
QUANTITIES = 25
VMEM_BYTES = 48 * 1024 * 1024
ALL_VMEM_BYTES = 63 * 1024 * 1024


def in_vmem(count):
    return [pl.BlockSpec(memory_space=pltpu.VMEM)] * count


def in_smem():
    return pl.BlockSpec(memory_space=pltpu.SMEM)


def params(vmem_bytes=VMEM_BYTES):
    return pltpu.CompilerParams(vmem_limit_bytes=vmem_bytes)


def is_even():
    return lax.axis_index("gx") % 2 == 0


def across(n):
    return [(i, (i + 1) % n if i % 2 else (i - 1) % n) for i in range(n)]


def within(n):
    return [(i, i ^ 1) for i in range(n)]


def swap_x(to_within, to_across):
    n = lax.axis_size("gx")
    got_across = lax.ppermute(to_across, "gx", across(n))
    got_within = lax.ppermute(to_within, "gx", within(n))
    return got_within, got_across


def m4_weights(offset):
    remain = 1.0 - offset
    return (
        -0.5 * offset * remain * remain,
        1.0 - 2.5 * offset * offset + 1.5 * offset * offset * offset,
        1.0 - 2.5 * remain * remain + 1.5 * remain * remain * remain,
        -0.5 * offset * offset * remain,
    )


def prepare(cells, offsets, strengths, table, rows):
    weight_x, weight_y, weight_z = (m4_weights(offset) for offset in offsets)
    cell_x = cells // (CY * NZ)
    cell_y = cells // NZ % CY
    cell_z = cells % NZ
    for plane in range(PLANES):
        along = jnp.zeros_like(offsets[0])
        for tap in range(4):
            along = jnp.where(cell_x == plane - tap, weight_x[tap], along)
        table[plane, rows] = along
    table[11, rows] = (cell_y - 1).astype(F32)
    table[12, rows] = ((cell_z - 1) & (NZ - 1)).astype(F32)
    for tap in range(4):
        table[7 + tap, rows] = weight_y[tap]
        for comp in range(3):
            table[13 + tap * 3 + comp, rows] = weight_z[tap] * strengths[comp]


def spread(table, first, tiles, planes, lines):
    ids = lax.broadcasted_iota(jnp.int32, (8, 128), 0)
    zero = jnp.zeros((8, 128), F32)
    half = lax.broadcasted_iota(jnp.int32, (16, 128), 0) // 8
    none = jnp.zeros((16, 128), BF16)
    for tile in range(tiles):
        lanes = slice(tile * 128, (tile + 1) * 128)

        def figure(k):
            return table[k, pl.ds(first + tile, 1)]

        first_row = figure(11).astype(jnp.int32)
        tap_of = (ids - first_row) & 7
        row = first_row + tap_of
        row_tile = jnp.where(row < 0, CY // 8, row >> 3)
        taps = zero
        for tap in range(4):
            taps = jnp.where(tap_of == tap, figure(7 + tap), taps)
        along_y = [jnp.where(row_tile == k, taps, 0.0) for k in range(ROWS // 8)]
        parts = [figure(plane) * piece for plane in range(PLANES) for piece in along_y]
        parts += [zero] * ((SPREAD - PLANES * ROWS) // 8)
        planes[:, lanes] = jnp.concatenate(parts, axis=0).astype(BF16)

        first_z = figure(12).astype(jnp.int32)
        tap_of = (ids - first_z) & 7
        z_tile = (((first_z + tap_of) & (NZ - 1)) >> 3).astype(F32)
        where_tap = [tap_of == tap for tap in range(4)]
        pair = (jnp.concatenate([z_tile, z_tile], axis=0) - half.astype(F32)).astype(BF16)
        doubled = []
        for comp in range(3):
            taps = zero
            for tap in range(4):
                taps = jnp.where(where_tap[tap], figure(13 + tap * 3 + comp), taps)
            doubled.append(jnp.concatenate([taps, taps], axis=0).astype(BF16))
        for k in range(NZ // 16):
            here = pair == jnp.asarray(2.0 * k, BF16)
            for comp in range(3):
                start = comp * NZ + 16 * k
                lines[start : start + 16, lanes] = jnp.where(here, doubled[comp], none)


def product(planes, lines):
    return lax.dot_general(
        planes[...], lines[...], (((1,), (1,)), ((), ())), preferred_element_type=F32
    )


def leaving_kernel(
    moving, cell_hbm, offset_hbm, vort_hbm, to_within, to_across, cells, offsets, vorts, packed, sems, *, capacity
):
    room = 2 * capacity
    copies = [
        pltpu.make_async_copy(offset_hbm.at[:, pl.ds(0, room)], offsets, sems.at[0]),
        pltpu.make_async_copy(vort_hbm.at[:, pl.ds(0, room)], vorts, sems.at[1]),
        pltpu.make_async_copy(cell_hbm.at[pl.ds(0, room // 128)], cells, sems.at[2]),
    ]
    for copy in copies:
        copy.start()
    even = is_even()
    prev_count = moving[0, 0]
    next_count = moving[0, 1]
    for copy in copies:
        copy.wait()
    packed[0:3] = offsets[...]
    packed[3:6] = vorts[...]
    for tile in range(room // 128):
        packed[6:7, tile * 128 : (tile + 1) * 128] = cells[tile : tile + 1].astype(F32)
    packed[7:8] = jnp.zeros((1, room), F32)
    ids = lax.broadcasted_iota(jnp.int32, (8, capacity), 1)
    listed = packed[...]
    shifted = pltpu.roll(listed, (room - prev_count) % room, 1)
    for_prev = jnp.where(ids < prev_count, listed[:, :capacity], 0.0)
    for_next = jnp.where(ids < next_count, shifted[:, :capacity], 0.0)
    to_within[...] = jnp.where(even, for_next, for_prev)
    to_across[...] = jnp.where(even, for_prev, for_next)


def particle_specs():
    return [in_smem()] + [pl.BlockSpec(memory_space=pl.ANY)] * 3


def pack_leaving(moving, cells, part_offset, part_vort):
    slots = part_offset.shape[1]
    capacity = slots // 17
    room = 2 * capacity
    message = jax.ShapeDtypeStruct((8, capacity), F32)
    return pl.pallas_call(
        functools.partial(leaving_kernel, capacity=capacity),
        in_specs=particle_specs(),
        out_specs=tuple(in_vmem(2)),
        out_shape=(message, message),
        scratch_shapes=[
            pltpu.VMEM((room // 128, 128), jnp.int32),
            pltpu.VMEM((3, room), F32),
            pltpu.VMEM((3, room), F32),
            pltpu.VMEM((8, room), F32),
            pltpu.SemaphoreType.DMA((3,)),
        ],
        compiler_params=params(ALL_VMEM_BYTES),
    )(moving, cells, part_offset, part_vort)


def staying_kernel(
    moving, cells, offsets, vorts, total, dense, table, planes_a, lines_a, planes_b, lines_b, *, tiles_per_chunk
):
    first_stay = moving[0, 0] + moving[0, 1]
    live_len = moving[0, 2]
    tiles = cells.shape[0]
    total[...] = jnp.zeros_like(total)
    for tile in range(tiles):
        lanes = slice(tile * 128, (tile + 1) * 128)
        for dim in range(3):
            dense[dim, tile : tile + 1] = offsets[dim : dim + 1, lanes]
            dense[3 + dim, tile : tile + 1] = vorts[dim : dim + 1, lanes]

    def one_group(group, carry):
        rows = pl.ds(pl.multiple_of(group * 8, 8), 8)
        slot = (
            group * 1024
            + lax.broadcasted_iota(jnp.int32, (8, 128), 0) * 128
            + lax.broadcasted_iota(jnp.int32, (8, 128), 1)
        )
        keep = (slot >= first_stay) & (slot < live_len)
        prepare(
            cells[rows],
            [dense[dim, rows] for dim in range(3)],
            [jnp.where(keep, dense[3 + dim, rows], 0.0) for dim in range(3)],
            table,
            rows,
        )
        return carry

    lax.fori_loop(0, tiles // 8, one_group, 0)
    chunks = tiles // tiles_per_chunk
    spread(table, 0, tiles_per_chunk, planes_a, lines_a)

    def two_chunks(pair, carry):
        spread(table, (2 * pair + 1) * tiles_per_chunk, tiles_per_chunk, planes_b, lines_b)
        total[...] += product(planes_a, lines_a)
        spread(table, (2 * pair + 2) * tiles_per_chunk, tiles_per_chunk, planes_a, lines_a)
        total[...] += product(planes_b, lines_b)
        return carry

    lax.fori_loop(0, (chunks - 1) // 2, two_chunks, 0)
    if chunks % 2 == 0:
        spread(table, (chunks - 1) * tiles_per_chunk, tiles_per_chunk, planes_b, lines_b)
        total[...] += product(planes_a, lines_a)
        total[...] += product(planes_b, lines_b)
    else:
        total[...] += product(planes_a, lines_a)


def deposit_staying(moving, cells, part_offset, part_vort):
    tiles = cells.shape[0]
    slots = tiles * 128
    per_chunk = 17
    chunk = per_chunk * 128
    return pl.pallas_call(
        functools.partial(staying_kernel, tiles_per_chunk=per_chunk),
        in_specs=[in_smem()] + in_vmem(3),
        out_specs=in_vmem(1)[0],
        out_shape=jax.ShapeDtypeStruct((SPREAD, 3 * NZ), F32),
        scratch_shapes=[
            pltpu.VMEM((6, tiles, 128), F32),
            pltpu.VMEM((QUANTITIES, tiles, 128), F32),
        ]
        + [pltpu.VMEM((SPREAD, chunk), BF16), pltpu.VMEM((3 * NZ, chunk), BF16)] * 2,
        compiler_params=params(),
        cost_estimate=pl.CostEstimate(
            flops=2 * SPREAD * 3 * NZ * slots, bytes_accessed=28 * slots, transcendentals=0
        ),
    )(moving, cells, part_offset, part_vort)


def arrived_kernel(total, got_within, got_across, deposits, to_within, to_across, dense, table, planes, lines):
    tiles = got_within.shape[1] // 128
    for which, got in enumerate((got_within, got_across)):
        for tile in range(tiles):
            lanes = slice(tile * 128, (tile + 1) * 128)
            place = which * tiles + tile
            for k in range(7):
                dense[k, place : place + 1] = got[k : k + 1, lanes]
    for group in range(2 * tiles // 8):
        rows = slice(group * 8, (group + 1) * 8)
        prepare(
            dense[6, rows].astype(jnp.int32),
            [dense[dim, rows] for dim in range(3)],
            [dense[3 + dim, rows] for dim in range(3)],
            table,
            rows,
        )
    spread(table, 0, 2 * tiles, planes, lines)
    whole = total[...] + product(planes, lines)
    for comp in range(3):
        for plane in range(PLANES):
            deposits[comp, plane] = whole[
                plane * ROWS : (plane + 1) * ROWS, comp * NZ : (comp + 1) * NZ
            ]
    even = is_even()
    first_within = jnp.where(even, CX, 0)
    first_across = jnp.where(even, 0, CX)
    to_within[...] = deposits[:, pl.ds(first_within, 3)]
    to_across[...] = deposits[:, pl.ds(first_across, 3)]


def deposit_arrived(total, got_within, got_across):
    received = got_within.shape[1]
    edge = jax.ShapeDtypeStruct((3, 3, ROWS, NZ), F32)
    tiles = 2 * received // 128
    return pl.pallas_call(
        arrived_kernel,
        in_specs=in_vmem(3),
        out_specs=tuple(in_vmem(3)),
        out_shape=(jax.ShapeDtypeStruct((3, PLANES, ROWS, NZ), F32), edge, edge),
        scratch_shapes=[
            pltpu.VMEM((7, tiles, 128), F32),
            pltpu.VMEM((QUANTITIES, tiles, 128), F32),
            pltpu.VMEM((SPREAD, 2 * received), BF16),
            pltpu.VMEM((3 * NZ, 2 * received), BF16),
        ],
        compiler_params=params(),
    )(total, got_within, got_across)


def edge_rows(low, high):
    ids = lax.broadcasted_iota(jnp.int32, (8, NZ), 0)
    return jnp.where(ids < 4, low, high)


def edged_plane(mine, other):
    return jnp.concatenate([mine, edge_rows(other[:8], other[-8:])], axis=0)


def roll_rows(value, shift):
    return pltpu.roll(value, shift % value.shape[0], 0)


def roll_z(value, shift):
    return pltpu.roll(value, shift % NZ, 1)


def relax(fields, sources):
    ids = lax.broadcasted_iota(jnp.int32, (ROWS, NZ), 0)
    frozen = (ids > CY) & (ids < ROWS - 1)
    for sweep in range(SWEEPS):
        fresh = list(fields)
        last = sweep == SWEEPS - 1
        for x in range(2 if last else 1, CX + (2 if last else 3)):
            centre = fields[x]
            summed = fields[x - 1] + fields[x + 1] + roll_rows(centre, 1) + roll_rows(centre, -1)
            summed = summed + roll_z(centre, 1) + roll_z(centre, -1) + sources[x - 1]
            fresh[x] = jnp.where(frozen, centre, summed * (1.0 / 6.0))
        fields = fresh
    return fields[2 : CX + 2]


def pack_rows(a, b, rows):
    ids = lax.broadcasted_iota(jnp.int32, (8, NZ), 0)
    first, last = b[:8], b[CY - 8 :]
    if rows == CY + 8:
        return jnp.concatenate([a, jnp.where(ids < 4, first, last)], axis=0)
    if rows == CY + 16:
        return jnp.concatenate([a, first, last], axis=0)
    middle = jnp.where(ids < 4, b[8:16], b[CY - 16 : CY - 8])
    return jnp.concatenate([a, first, middle, last], axis=0)


def unpack_rows(packed):
    a, rest = packed[:CY], packed[CY:]
    first, last = rest[:8], rest[rest.shape[0] - 8 :]
    middle = rest[8:16] if rest.shape[0] == 24 else last
    return a, jnp.concatenate([first, middle, middle, last], axis=0)


def hand_out(potential, to_within, to_across):
    even = is_even()
    rows = to_within.shape[2]
    for comp in range(3):
        for x in range(2):
            low, high = (
                pack_rows(potential[comp, at, :CY], potential[comp, at, CY:], rows)
                for at in (x, CX - 2 + x)
            )
            to_within[comp, x] = jnp.where(even, high, low)
            to_across[comp, x] = jnp.where(even, low, high)


def fold_kernel(deposits, got_within, got_across, mine, message):
    even = is_even()
    ids = lax.broadcasted_iota(jnp.int32, (8, NZ), 0)
    for comp in range(3):
        for x in range(CX + 2):
            value = deposits[comp, x]
            if x < 3:
                value = value + jnp.where(even, got_across[comp, x], got_within[comp, x])
            if x >= CX:
                value = value + jnp.where(even, got_within[comp, x - CX], got_across[comp, x - CX])
            mine[comp, x] = value
            edges = value[CY:]
            third = jnp.where(ids < 2, edges, jnp.where(ids == 2, roll_rows(edges, 3), value[16:24]))
            message[comp, x] = jnp.concatenate([value[:16], third, value[24:CY]], axis=0)


def first_kernel(mine, other, omega, potential, to_within, to_across):
    ids = lax.broadcasted_iota(jnp.int32, (8, NZ), 0)

    def folded(main, edges):
        low = main[:8] + jnp.where(ids < 2, edges, 0.0)
        high = main[CY - 8 : CY] + jnp.where(ids == 7, edges, 0.0)
        return jnp.concatenate([low, main[8 : CY - 8], high], axis=0)

    def one_component(comp, carry):
        sources = ([], [])
        for x in range(CX + 2):
            a = mine[comp, x]
            b = other[comp, x]
            third = b[16:24]
            b_edges = jnp.where(ids < 2, third, roll_rows(third, 5))
            omega_a = folded(a[:CY], b_edges)
            omega_b = folded(b, a[CY:])
            omega[comp, x, :CY] = omega_a
            omega[comp, x, CY:] = omega_b
            sources[0].append(edged_plane(omega_a, omega_b))
            sources[1].append(edged_plane(omega_b, omega_a))
        for block in range(2):
            fields = [jnp.zeros((ROWS, NZ), F32)] * (CX + 4)
            fields = relax(fields, sources[block])
            for x in range(CX):
                potential[comp, x, block * CY : (block + 1) * CY] = fields[x][:CY]
        return carry

    lax.fori_loop(0, 3, one_component, 0)
    hand_out(potential, to_within, to_across)


def gathered(potential, got_within, got_across, comp):
    even = is_even()

    def chosen(pick, x):
        return unpack_rows(jnp.where(pick, got_within[comp, x], got_across[comp, x]))

    below = [chosen(jnp.logical_not(even), x) for x in range(2)]
    above = [chosen(even, x) for x in range(2)]
    middle = [(potential[comp, x, :CY], potential[comp, x, CY:]) for x in range(CX)]
    return below + middle + above


def next_kernel(omega, before, got_within, got_across, potential, to_within, to_across):
    def one_component(comp, carry):
        pairs = gathered(before, got_within, got_across, comp)
        charge = [(omega[comp, x, :CY], omega[comp, x, CY:]) for x in range(CX + 2)]
        for block in range(2):
            fields = [edged_plane(pair[block], pair[1 - block]) for pair in pairs]
            sources = [edged_plane(pair[block], pair[1 - block]) for pair in charge]
            fields = relax(fields, sources)
            for x in range(CX):
                potential[comp, x, block * CY : (block + 1) * CY] = fields[x][:CY]
        return carry

    lax.fori_loop(0, 3, one_component, 0)
    hand_out(potential, to_within, to_across)


def last_kernel(omega, potential, got_within, got_across, velocity, stretching):
    psi = []
    for comp in range(3):
        pairs = gathered(potential, got_within, got_across, comp)
        psi.append([edged_plane(a, b) for a, b in pairs])

    def slope_x(planes, x):
        return (planes[x + 1] - planes[x - 1]) * 0.5

    def slope_y(plane):
        return (roll_rows(plane, -1) - roll_rows(plane, 1)) * 0.5

    def slope_z(plane):
        return (roll_z(plane, -1) - roll_z(plane, 1)) * 0.5

    speeds = ([None], [None], [None])
    for x in range(1, CX + 3):
        speeds[0].append(slope_y(psi[2][x]) - slope_z(psi[1][x]))
        speeds[1].append(slope_z(psi[0][x]) - slope_x(psi[2], x))
        speeds[2].append(slope_x(psi[1], x) - slope_y(psi[0][x]))
    for comp in range(3):
        for x in range(CX):
            centre = speeds[comp][x + 2]
            velocity[comp, x] = centre[:CY]
            stretching[comp, x] = (
                omega[0, x + 1, :CY] * slope_x(speeds[comp], x + 2)[:CY]
                + omega[1, x + 1, :CY] * slope_y(centre)[:CY]
                + omega[2, x + 1, :CY] * slope_z(centre)[:CY]
            )


def array(*shape):
    return jax.ShapeDtypeStruct(shape, F32)


def on_vmem(kernel, outs, *args):
    return pl.pallas_call(
        kernel,
        in_specs=in_vmem(len(args)),
        out_specs=tuple(in_vmem(len(outs))),
        out_shape=outs,
        compiler_params=params(),
    )(*args)


def two_block_solve(deposits, to_within, to_across):
    planes = CX + 2
    mine, message = on_vmem(
        fold_kernel,
        (array(3, planes, ROWS, NZ), array(3, planes, CY, NZ)),
        deposits,
        *swap_x(to_within, to_across),
    )
    other = lax.ppermute(message, "gy", [(0, 1), (1, 0)])
    slab = array(3, CX, 2 * CY, NZ)
    depths = [CY + 24, CY + 16, CY + 16, CY + 8]
    edge = array(3, 2, depths[0], NZ)
    omega, potential, to_within, to_across = on_vmem(
        first_kernel, (array(3, planes, 2 * CY, NZ), slab, edge, edge), mine, other
    )
    for depth in depths[1:]:
        edge = array(3, 2, depth, NZ)
        potential, to_within, to_across = on_vmem(
            next_kernel, (slab, edge, edge), omega, potential, *swap_x(to_within, to_across)
        )
    block = array(3, CX, CY, NZ)
    return on_vmem(
        last_kernel, (block, block), omega, potential, *swap_x(to_within, to_across)
    )


def padded(value, sides, width):
    for axis, dim in sides:
        devices, length = (lax.axis_size(axis), value.shape[dim])
        up = [(i, (i + 1) % devices) for i in range(devices)]
        down = [(j, i) for i, j in up]
        last = lax.slice_in_dim(value, length - width, length, axis=dim)
        leading = lax.slice_in_dim(value, 0, width, axis=dim)
        before = lax.ppermute(last, axis, up)
        after = lax.ppermute(leading, axis, down)
        value = jnp.concatenate([before, value, after], axis=dim)
    return value


def jacobi_sweep(field, source):
    centre = field[..., 1:-1, 1:-1, :]
    summed = (
        field[..., :-2, 1:-1, :]
        + field[..., 2:, 1:-1, :]
        + field[..., 1:-1, :-2, :]
        + field[..., 1:-1, 2:, :]
    )
    summed = summed + jnp.roll(centre, 1, -1) + jnp.roll(centre, -1, -1) + source
    return field.at[..., 1:-1, 1:-1, :].set(summed / 6.0)


def slope_x(field):
    return (field[2:, 1:-1] - field[:-2, 1:-1]) * 0.5


def slope_y(field):
    return (field[1:-1, 2:] - field[1:-1, :-2]) * 0.5


def slope_z(field):
    centre = field[1:-1, 1:-1]
    return (jnp.roll(centre, -1, -1) - jnp.roll(centre, 1, -1)) * 0.5


def fold_ghosts(extended, axis_dim, extent):
    centre = lax.slice_in_dim(extended, 4, extent + 4, axis=axis_dim)
    low_rim = lax.slice_in_dim(extended, 0, 2, axis=axis_dim)
    high_rim = lax.slice_in_dim(extended, extent + 6, extent + 8, axis=axis_dim)
    pad_low = [(0, 0)] * extended.ndim
    pad_high = [(0, 0)] * extended.ndim
    pad_low[axis_dim] = (0, extent - 2)
    pad_high[axis_dim] = (extent - 2, 0)
    return centre + jnp.pad(low_rim, pad_low) + jnp.pad(high_rim, pad_high)


def general_solve(deposits):
    sides = (("gx", 1), ("gy", 2))
    rows = jnp.concatenate(
        [jnp.zeros_like(deposits[:, :, :1]), deposits[:, :, ROWS - 1 :], deposits[:, :, : CY + 2]],
        axis=2,
    )
    full = jnp.pad(rows, ((0, 0), (1, 0), (0, 0), (0, 0)))
    omega = fold_ghosts(fold_ghosts(padded(full, sides, 2), 1, CX), 2, CY)
    source = padded(omega, sides, 2)[:, 1:-1, 1:-1]
    potential = jnp.zeros_like(omega)
    for _ in range(OUTER):
        field = padded(potential, sides, 2)
        for _ in range(SWEEPS):
            field = jacobi_sweep(field, source)
        potential = field[:, 2:-2, 2:-2]
    wide = padded(potential, sides, 2)
    edged_velocity = jnp.stack(
        [
            slope_y(wide[2]) - slope_z(wide[1]),
            slope_z(wide[0]) - slope_x(wide[2]),
            slope_x(wide[1]) - slope_y(wide[0]),
        ]
    )
    stretching = jnp.stack(
        [
            omega[0] * slope_x(edged_velocity[comp])
            + omega[1] * slope_y(edged_velocity[comp])
            + omega[2] * slope_z(edged_velocity[comp])
            for comp in range(3)
        ]
    )
    return edged_velocity[:, 1:-1, 1:-1], stretching


def per_device(part_cell, part_offset, part_vort, moving):
    particles = (moving, part_cell.reshape(-1, 128), part_offset, part_vort)
    got_within, got_across = swap_x(*pack_leaving(*particles))
    total = deposit_staying(*particles)
    deposits, to_within, to_across = deposit_arrived(total, got_within, got_across)
    if lax.axis_size("gy") == 2:
        return two_block_solve(deposits, to_within, to_across)
    return general_solve(deposits)


def solution(mesh):
    return jax.shard_map(
        per_device,
        mesh=mesh,
        in_specs=(
            P(("gx", "gy")),
            P(None, ("gx", "gy")),
            P(None, ("gx", "gy")),
            P(("gx", "gy"), None),
        ),
        out_specs=(P(None, "gx", "gy", None), P(None, "gx", "gy", None)),
        check_vma=False,
    )
```

```python
import functools

import jax
import jax.numpy as jnp
from jax import lax
from jax.experimental import pallas as pl
from jax.experimental.pallas import tpu as pltpu
from jax.sharding import PartitionSpec as P

CX = 4
CY = 32
NZ = 128
OUTER = 4
SWEEPS = 3
F32 = jnp.float32
BF16 = jnp.bfloat16
ROWS = CY + 8
PLANES = CX + 3
SPREAD = 288
QUANTITIES = 25
VMEM_BYTES = 48 * 1024 * 1024
ALL_VMEM_BYTES = 63 * 1024 * 1024


def in_vmem(count):
    return [pl.BlockSpec(memory_space=pltpu.VMEM)] * count


def in_smem():
    return pl.BlockSpec(memory_space=pltpu.SMEM)


def params(vmem_bytes=VMEM_BYTES):
    return pltpu.CompilerParams(vmem_limit_bytes=vmem_bytes)


def is_even():
    return lax.axis_index("gx") % 2 == 0


def across(n):
    return [(i, (i + 1) % n if i % 2 else (i - 1) % n) for i in range(n)]


def within(n):
    return [(i, i ^ 1) for i in range(n)]


def swap_x(to_within, to_across):
    n = lax.axis_size("gx")
    got_across = lax.ppermute(to_across, "gx", across(n))
    got_within = lax.ppermute(to_within, "gx", within(n))
    return got_within, got_across


def m4_weights(offset):
    remain = 1.0 - offset
    return (
        -0.5 * offset * remain * remain,
        1.0 - 2.5 * offset * offset + 1.5 * offset * offset * offset,
        1.0 - 2.5 * remain * remain + 1.5 * remain * remain * remain,
        -0.5 * offset * offset * remain,
    )


def prepare(cells, offsets, strengths, table, rows):
    weight_x, weight_y, weight_z = (m4_weights(offset) for offset in offsets)
    cell_x = cells // (CY * NZ)
    cell_y = cells // NZ % CY
    cell_z = cells % NZ
    for plane in range(PLANES):
        along = jnp.zeros_like(offsets[0])
        for tap in range(4):
            along = jnp.where(cell_x == plane - tap, weight_x[tap], along)
        table[plane, rows] = along
    table[11, rows] = (cell_y - 1).astype(F32)
    table[12, rows] = ((cell_z - 1) & (NZ - 1)).astype(F32)
    for tap in range(4):
        table[7 + tap, rows] = weight_y[tap]
        for comp in range(3):
            table[13 + tap * 3 + comp, rows] = weight_z[tap] * strengths[comp]


def spread(table, first, tiles, planes, lines):
    ids = lax.broadcasted_iota(jnp.int32, (8, 128), 0)
    zero = jnp.zeros((8, 128), F32)
    half = lax.broadcasted_iota(jnp.int32, (16, 128), 0) // 8
    none = jnp.zeros((16, 128), BF16)
    for tile in range(tiles):
        lanes = slice(tile * 128, (tile + 1) * 128)

        def figure(k):
            return table[k, pl.ds(first + tile, 1)]

        first_row = figure(11).astype(jnp.int32)
        tap_of = (ids - first_row) & 7
        row = first_row + tap_of
        row_tile = jnp.where(row < 0, CY // 8, row >> 3)
        taps = zero
        for tap in range(4):
            taps = jnp.where(tap_of == tap, figure(7 + tap), taps)
        along_y = [jnp.where(row_tile == k, taps, 0.0) for k in range(ROWS // 8)]
        parts = [figure(plane) * piece for plane in range(PLANES) for piece in along_y]
        parts += [zero] * ((SPREAD - PLANES * ROWS) // 8)
        planes[:, lanes] = jnp.concatenate(parts, axis=0).astype(BF16)

        first_z = figure(12).astype(jnp.int32)
        tap_of = (ids - first_z) & 7
        z_tile = (((first_z + tap_of) & (NZ - 1)) >> 3).astype(F32)
        where_tap = [tap_of == tap for tap in range(4)]
        pair = (jnp.concatenate([z_tile, z_tile], axis=0) - half.astype(F32)).astype(BF16)
        doubled = []
        for comp in range(3):
            taps = zero
            for tap in range(4):
                taps = jnp.where(where_tap[tap], figure(13 + tap * 3 + comp), taps)
            doubled.append(jnp.concatenate([taps, taps], axis=0).astype(BF16))
        for k in range(NZ // 16):
            here = pair == jnp.asarray(2.0 * k, BF16)
            for comp in range(3):
                start = comp * NZ + 16 * k
                lines[start : start + 16, lanes] = jnp.where(here, doubled[comp], none)


def product(planes, lines):
    return lax.dot_general(
        planes[...], lines[...], (((1,), (1,)), ((), ())), preferred_element_type=F32
    )


def leaving_kernel(
    moving, cell_hbm, offset_hbm, vort_hbm, to_within, to_across, cells, offsets, vorts, packed, sems, *, capacity
):
    room = 2 * capacity
    copies = [
        pltpu.make_async_copy(offset_hbm.at[:, pl.ds(0, room)], offsets, sems.at[0]),
        pltpu.make_async_copy(vort_hbm.at[:, pl.ds(0, room)], vorts, sems.at[1]),
        pltpu.make_async_copy(cell_hbm.at[pl.ds(0, room // 128)], cells, sems.at[2]),
    ]
    for copy in copies:
        copy.start()
    even = is_even()
    prev_count = moving[0, 0]
    next_count = moving[0, 1]
    for copy in copies:
        copy.wait()
    packed[0:3] = offsets[...]
    packed[3:6] = vorts[...]
    for tile in range(room // 128):
        packed[6:7, tile * 128 : (tile + 1) * 128] = cells[tile : tile + 1].astype(F32)
    packed[7:8] = jnp.zeros((1, room), F32)
    ids = lax.broadcasted_iota(jnp.int32, (8, capacity), 1)
    listed = packed[...]
    shifted = pltpu.roll(listed, (room - prev_count) % room, 1)
    for_prev = jnp.where(ids < prev_count, listed[:, :capacity], 0.0)
    for_next = jnp.where(ids < next_count, shifted[:, :capacity], 0.0)
    to_within[...] = jnp.where(even, for_next, for_prev)
    to_across[...] = jnp.where(even, for_prev, for_next)


def particle_specs():
    return [in_smem()] + [pl.BlockSpec(memory_space=pl.ANY)] * 3


def pack_leaving(moving, cells, part_offset, part_vort):
    slots = part_offset.shape[1]
    capacity = slots // 17
    room = 2 * capacity
    message = jax.ShapeDtypeStruct((8, capacity), F32)
    return pl.pallas_call(
        functools.partial(leaving_kernel, capacity=capacity),
        in_specs=particle_specs(),
        out_specs=tuple(in_vmem(2)),
        out_shape=(message, message),
        scratch_shapes=[
            pltpu.VMEM((room // 128, 128), jnp.int32),
            pltpu.VMEM((3, room), F32),
            pltpu.VMEM((3, room), F32),
            pltpu.VMEM((8, room), F32),
            pltpu.SemaphoreType.DMA((3,)),
        ],
        compiler_params=params(ALL_VMEM_BYTES),
    )(moving, cells, part_offset, part_vort)


def staying_kernel(
    moving, cells, offsets, vorts, total, dense, table, planes_a, lines_a, planes_b, lines_b, *, per_chunk
):
    first_stay = moving[0, 0] + moving[0, 1]
    live_len = moving[0, 2]
    tiles = cells.shape[0]
    chunks = tiles // per_chunk
    total[...] = jnp.zeros_like(total)

    def make(chunk, count, planes, lines):
        first = pl.multiple_of(chunk * per_chunk, 8)
        for tile in range(count):
            lanes = pl.ds(pl.multiple_of((first + tile) * 128, 128), 128)
            for dim in range(3):
                dense[dim, tile : tile + 1] = offsets[dim : dim + 1, lanes]
                dense[3 + dim, tile : tile + 1] = vorts[dim : dim + 1, lanes]
        slot = lax.broadcasted_iota(jnp.int32, (8, 128), 0) * 128
        slot = slot + lax.broadcasted_iota(jnp.int32, (8, 128), 1)
        for group in range(count // 8):
            rows = slice(group * 8, (group + 1) * 8)
            own_slot = slot + (first + group * 8) * 128
            keep = (own_slot >= first_stay) & (own_slot < live_len)
            prepare(
                cells[pl.ds(pl.multiple_of(first + group * 8, 8), 8)],
                [dense[dim, rows] for dim in range(3)],
                [jnp.where(keep, dense[3 + dim, rows], 0.0) for dim in range(3)],
                table,
                rows,
            )
        spread(table, 0, count, planes, lines)

    make(0, per_chunk, planes_a, lines_a)

    def two_chunks(pair, carry):
        make(2 * pair + 1, per_chunk, planes_b, lines_b)
        total[...] += product(planes_a, lines_a)
        make(2 * pair + 2, per_chunk, planes_a, lines_a)
        total[...] += product(planes_b, lines_b)
        return carry

    lax.fori_loop(0, (chunks - 1) // 2, two_chunks, 0)
    done, spare = (planes_a, lines_a), (planes_b, lines_b)
    if chunks % 2 == 0:
        make(chunks - 1, per_chunk, *spare)
        total[...] += product(*done)
        done, spare = spare, done
    rest = tiles % per_chunk
    if rest:
        make(chunks, rest, *spare)
        total[...] += product(*done)
        done = tuple(ref.at[:, : rest * 128] for ref in spare)
    total[...] += product(*done)


def deposit_staying(moving, cells, part_offset, part_vort):
    tiles = cells.shape[0]
    slots = tiles * 128
    per_chunk = 16
    chunk = per_chunk * 128
    return pl.pallas_call(
        functools.partial(staying_kernel, per_chunk=per_chunk),
        in_specs=[in_smem()] + in_vmem(3),
        out_specs=in_vmem(1)[0],
        out_shape=jax.ShapeDtypeStruct((SPREAD, 3 * NZ), F32),
        scratch_shapes=[
            pltpu.VMEM((6, per_chunk, 128), F32),
            pltpu.VMEM((QUANTITIES, per_chunk, 128), F32),
        ]
        + [pltpu.VMEM((SPREAD, chunk), BF16), pltpu.VMEM((3 * NZ, chunk), BF16)] * 2,
        compiler_params=params(),
        cost_estimate=pl.CostEstimate(
            flops=2 * SPREAD * 3 * NZ * slots, bytes_accessed=28 * slots, transcendentals=0
        ),
    )(moving, cells, part_offset, part_vort)


def arrived_kernel(total, got_within, got_across, deposits, to_within, to_across, dense, table, planes, lines):
    tiles = got_within.shape[1] // 128
    for which, got in enumerate((got_within, got_across)):
        for tile in range(tiles):
            lanes = slice(tile * 128, (tile + 1) * 128)
            place = which * tiles + tile
            for k in range(7):
                dense[k, place : place + 1] = got[k : k + 1, lanes]
    for group in range(2 * tiles // 8):
        rows = slice(group * 8, (group + 1) * 8)
        prepare(
            dense[6, rows].astype(jnp.int32),
            [dense[dim, rows] for dim in range(3)],
            [dense[3 + dim, rows] for dim in range(3)],
            table,
            rows,
        )
    spread(table, 0, 2 * tiles, planes, lines)
    whole = total[...] + product(planes, lines)
    for comp in range(3):
        for plane in range(PLANES):
            deposits[comp, plane] = whole[
                plane * ROWS : (plane + 1) * ROWS, comp * NZ : (comp + 1) * NZ
            ]
    even = is_even()
    first_within = jnp.where(even, CX, 0)
    first_across = jnp.where(even, 0, CX)
    to_within[...] = deposits[:, pl.ds(first_within, 3)]
    to_across[...] = deposits[:, pl.ds(first_across, 3)]


def deposit_arrived(total, got_within, got_across):
    received = got_within.shape[1]
    edge = jax.ShapeDtypeStruct((3, 3, ROWS, NZ), F32)
    tiles = 2 * received // 128
    return pl.pallas_call(
        arrived_kernel,
        in_specs=in_vmem(3),
        out_specs=tuple(in_vmem(3)),
        out_shape=(jax.ShapeDtypeStruct((3, PLANES, ROWS, NZ), F32), edge, edge),
        scratch_shapes=[
            pltpu.VMEM((7, tiles, 128), F32),
            pltpu.VMEM((QUANTITIES, tiles, 128), F32),
            pltpu.VMEM((SPREAD, 2 * received), BF16),
            pltpu.VMEM((3 * NZ, 2 * received), BF16),
        ],
        compiler_params=params(),
    )(total, got_within, got_across)


def edge_rows(low, high):
    ids = lax.broadcasted_iota(jnp.int32, (8, NZ), 0)
    return jnp.where(ids < 4, low, high)


def edged_plane(mine, other, ends_only=False):
    edges = edge_rows(other[:8], other[-8:])
    if ends_only:
        return jnp.concatenate([mine[-8:], edges, mine[:8]], axis=0)
    return jnp.concatenate([mine, edges], axis=0)


def roll_rows(value, shift):
    return pltpu.roll(value, shift % value.shape[0], 0)


def roll_z(value, shift):
    return pltpu.roll(value, shift % NZ, 1)


def relax(fields, sources):
    rows = fields[0].shape[0]
    first_edge = CY if rows == ROWS else 8
    ids = lax.broadcasted_iota(jnp.int32, (rows, NZ), 0)
    frozen = (ids > first_edge) & (ids < first_edge + 7)
    for sweep in range(SWEEPS):
        fresh = list(fields)
        last = sweep == SWEEPS - 1
        for x in range(2 if last else 1, CX + (2 if last else 3)):
            centre = fields[x]
            summed = fields[x - 1] + fields[x + 1] + roll_rows(centre, 1) + roll_rows(centre, -1)
            summed = summed + roll_z(centre, 1) + roll_z(centre, -1) + sources[x - 1]
            fresh[x] = jnp.where(frozen, centre, summed * (1.0 / 6.0))
        fields = fresh
    return fields[2 : CX + 2]


def pack_rows(value, rows):
    ids = lax.broadcasted_iota(jnp.int32, (8, NZ), 0)
    a, b = value[:CY], value[CY:]
    first, last = b[:8], b[-8:]
    if rows == CY + 8:
        return jnp.concatenate([a, jnp.where(ids < 4, first, last)], axis=0)
    if rows == CY + 16:
        return jnp.concatenate([a, first, last], axis=0)
    middle = jnp.where(ids < 4, b[8:16], b[CY - 16 : CY - 8])
    return jnp.concatenate([a, first, middle, last], axis=0)


def unpack_rows(packed):
    a, b = packed[:CY], packed[CY:]
    if b.shape[0] == 24:
        b = jnp.concatenate([b[:16], b[8:]], axis=0)
    return a, b


def hand_out(potential, to_within, to_across):
    even = is_even()
    rows = to_within.shape[2]
    for comp in range(3):
        for x in range(2):
            low, high = (pack_rows(potential[comp, at], rows) for at in (x, CX - 2 + x))
            to_within[comp, x] = jnp.where(even, high, low)
            to_across[comp, x] = jnp.where(even, low, high)


def fold_kernel(deposits, got_within, got_across, mine, message):
    even = is_even()
    ids = lax.broadcasted_iota(jnp.int32, (8, NZ), 0)
    for comp in range(3):
        for x in range(CX + 2):
            value = deposits[comp, x]
            if x < 3:
                value = value + jnp.where(even, got_across[comp, x], got_within[comp, x])
            if x >= CX:
                value = value + jnp.where(even, got_within[comp, x - CX], got_across[comp, x - CX])
            mine[comp, x] = value
            edges = value[CY:]
            third = jnp.where(ids < 2, edges, jnp.where(ids == 2, roll_rows(edges, 3), value[16:24]))
            message[comp, x] = jnp.concatenate([value[:16], third, value[24:CY]], axis=0)


def first_kernel(mine, other, omega, potential, to_within, to_across):
    ids = lax.broadcasted_iota(jnp.int32, (8, NZ), 0)

    def folded(main, edges):
        low = main[:8] + jnp.where(ids < 2, edges, 0.0)
        high = main[CY - 8 : CY] + jnp.where(ids == 7, edges, 0.0)
        return jnp.concatenate([low, main[8 : CY - 8], high], axis=0)

    for comp in range(3):
        sources = ([], [])
        for x in range(CX + 2):
            a = mine[comp, x]
            b = other[comp, x]
            third = b[16:24]
            b_edges = jnp.where(ids < 2, third, roll_rows(third, 5))
            omega_a = folded(a[:CY], b_edges)
            omega_b = folded(b, a[CY:])
            omega[comp, x, :CY] = omega_a
            omega[comp, x, CY:] = omega_b
            sources[0].append(edged_plane(omega_a, omega_b))
            sources[1].append(edged_plane(omega_b, omega_a))
        for block in range(2):
            fields = [jnp.zeros((ROWS, NZ), F32)] * (CX + 4)
            fields = relax(fields, sources[block])
            for x in range(CX):
                potential[comp, x, block * CY : (block + 1) * CY] = fields[x][:CY]
    hand_out(potential, to_within, to_across)


def gathered(potential, got_within, got_across, comp):
    even = is_even()

    def chosen(pick, x):
        return unpack_rows(jnp.where(pick, got_within[comp, x], got_across[comp, x]))

    below = [chosen(jnp.logical_not(even), x) for x in range(2)]
    above = [chosen(even, x) for x in range(2)]
    middle = [unpack_rows(potential[comp, x]) for x in range(CX)]
    return below + middle + above


def next_kernel(omega, before, got_within, got_across, potential, to_within, to_across):
    ends_only = before.shape[2] == CY + 16
    for comp in range(3):
        pairs = gathered(before, got_within, got_across, comp)
        charge = [(omega[comp, x, :CY], omega[comp, x, CY:]) for x in range(CX + 2)]
        fields = relax([edged_plane(a, b) for a, b in pairs], [edged_plane(a, b) for a, b in charge])
        for x in range(CX):
            potential[comp, x, :CY] = fields[x][:CY]
        fields = relax(
            [edged_plane(b, a, ends_only) for a, b in pairs],
            [edged_plane(b, a, ends_only) for a, b in charge],
        )
        first = 16 if ends_only else 0
        last = 0 if ends_only else CY - 8
        for x in range(CX):
            potential[comp, x, CY : CY + 8] = fields[x][first : first + 8]
            potential[comp, x, CY + 8 :] = fields[x][last : last + 8]
    hand_out(potential, to_within, to_across)


def last_kernel(omega, potential, got_within, got_across, velocity, stretching):
    psi = []
    for comp in range(3):
        pairs = gathered(potential, got_within, got_across, comp)
        psi.append([edged_plane(a, b) for a, b in pairs])

    def slope_x(planes, x):
        return (planes[x + 1] - planes[x - 1]) * 0.5

    def slope_y(plane):
        return (roll_rows(plane, -1) - roll_rows(plane, 1)) * 0.5

    def slope_z(plane):
        return (roll_z(plane, -1) - roll_z(plane, 1)) * 0.5

    speeds = ([None], [None], [None])
    for x in range(1, CX + 3):
        speeds[0].append(slope_y(psi[2][x]) - slope_z(psi[1][x]))
        speeds[1].append(slope_z(psi[0][x]) - slope_x(psi[2], x))
        speeds[2].append(slope_x(psi[1], x) - slope_y(psi[0][x]))
    for comp in range(3):
        for x in range(CX):
            centre = speeds[comp][x + 2]
            velocity[comp, x] = centre[:CY]
            stretching[comp, x] = (
                omega[0, x + 1, :CY] * slope_x(speeds[comp], x + 2)[:CY]
                + omega[1, x + 1, :CY] * slope_y(centre)[:CY]
                + omega[2, x + 1, :CY] * slope_z(centre)[:CY]
            )


def array(*shape):
    return jax.ShapeDtypeStruct(shape, F32)


def on_vmem(kernel, outs, *args):
    return pl.pallas_call(
        kernel,
        in_specs=in_vmem(len(args)),
        out_specs=tuple(in_vmem(len(outs))),
        out_shape=outs,
        compiler_params=params(),
    )(*args)


def two_block_solve(deposits, to_within, to_across):
    planes = CX + 2
    mine, message = on_vmem(
        fold_kernel,
        (array(3, planes, ROWS, NZ), array(3, planes, CY, NZ)),
        deposits,
        *swap_x(to_within, to_across),
    )
    other = lax.ppermute(message, "gy", [(0, 1), (1, 0)])
    whole, ends = array(3, CX, 2 * CY, NZ), array(3, CX, CY + 16, NZ)
    depths = [CY + 24, CY + 16, CY + 16, CY + 8]
    edge = array(3, 2, depths[0], NZ)
    omega, potential, to_within, to_across = on_vmem(
        first_kernel, (array(3, planes, 2 * CY, NZ), whole, edge, edge), mine, other
    )
    for depth in depths[1:]:
        edge = array(3, 2, depth, NZ)
        potential, to_within, to_across = on_vmem(
            next_kernel, (ends, edge, edge), omega, potential, *swap_x(to_within, to_across)
        )
    block = array(3, CX, CY, NZ)
    return on_vmem(
        last_kernel, (block, block), omega, potential, *swap_x(to_within, to_across)
    )


def padded(value, sides, width):
    for axis, dim in sides:
        devices, length = (lax.axis_size(axis), value.shape[dim])
        up = [(i, (i + 1) % devices) for i in range(devices)]
        down = [(j, i) for i, j in up]
        last = lax.slice_in_dim(value, length - width, length, axis=dim)
        leading = lax.slice_in_dim(value, 0, width, axis=dim)
        before = lax.ppermute(last, axis, up)
        after = lax.ppermute(leading, axis, down)
        value = jnp.concatenate([before, value, after], axis=dim)
    return value


def jacobi_sweep(field, source):
    centre = field[..., 1:-1, 1:-1, :]
    summed = (
        field[..., :-2, 1:-1, :]
        + field[..., 2:, 1:-1, :]
        + field[..., 1:-1, :-2, :]
        + field[..., 1:-1, 2:, :]
    )
    summed = summed + jnp.roll(centre, 1, -1) + jnp.roll(centre, -1, -1) + source
    return field.at[..., 1:-1, 1:-1, :].set(summed / 6.0)


def slope_x(field):
    return (field[2:, 1:-1] - field[:-2, 1:-1]) * 0.5


def slope_y(field):
    return (field[1:-1, 2:] - field[1:-1, :-2]) * 0.5


def slope_z(field):
    centre = field[1:-1, 1:-1]
    return (jnp.roll(centre, -1, -1) - jnp.roll(centre, 1, -1)) * 0.5


def fold_ghosts(extended, axis_dim, extent):
    centre = lax.slice_in_dim(extended, 4, extent + 4, axis=axis_dim)
    low_rim = lax.slice_in_dim(extended, 0, 2, axis=axis_dim)
    high_rim = lax.slice_in_dim(extended, extent + 6, extent + 8, axis=axis_dim)
    pad_low = [(0, 0)] * extended.ndim
    pad_high = [(0, 0)] * extended.ndim
    pad_low[axis_dim] = (0, extent - 2)
    pad_high[axis_dim] = (extent - 2, 0)
    return centre + jnp.pad(low_rim, pad_low) + jnp.pad(high_rim, pad_high)


def general_solve(deposits):
    sides = (("gx", 1), ("gy", 2))
    rows = jnp.concatenate(
        [jnp.zeros_like(deposits[:, :, :1]), deposits[:, :, ROWS - 1 :], deposits[:, :, : CY + 2]],
        axis=2,
    )
    full = jnp.pad(rows, ((0, 0), (1, 0), (0, 0), (0, 0)))
    omega = fold_ghosts(fold_ghosts(padded(full, sides, 2), 1, CX), 2, CY)
    source = padded(omega, sides, 2)[:, 1:-1, 1:-1]
    potential = jnp.zeros_like(omega)
    for _ in range(OUTER):
        field = padded(potential, sides, 2)
        for _ in range(SWEEPS):
            field = jacobi_sweep(field, source)
        potential = field[:, 2:-2, 2:-2]
    wide = padded(potential, sides, 2)
    edged_velocity = jnp.stack(
        [
            slope_y(wide[2]) - slope_z(wide[1]),
            slope_z(wide[0]) - slope_x(wide[2]),
            slope_x(wide[1]) - slope_y(wide[0]),
        ]
    )
    stretching = jnp.stack(
        [
            omega[0] * slope_x(edged_velocity[comp])
            + omega[1] * slope_y(edged_velocity[comp])
            + omega[2] * slope_z(edged_velocity[comp])
            for comp in range(3)
        ]
    )
    return edged_velocity[:, 1:-1, 1:-1], stretching


def per_device(part_cell, part_offset, part_vort, moving):
    particles = (moving, part_cell.reshape(-1, 128), part_offset, part_vort)
    got_within, got_across = swap_x(*pack_leaving(*particles))
    total = deposit_staying(*particles)
    deposits, to_within, to_across = deposit_arrived(total, got_within, got_across)
    if lax.axis_size("gy") == 2:
        return two_block_solve(deposits, to_within, to_across)
    return general_solve(deposits)


def solution(mesh):
    return jax.shard_map(
        per_device,
        mesh=mesh,
        in_specs=(
            P(("gx", "gy")),
            P(None, ("gx", "gy")),
            P(None, ("gx", "gy")),
            P(("gx", "gy"), None),
        ),
        out_specs=(P(None, "gx", "gy", None), P(None, "gx", "gy", None)),
        check_vma=False,
    )
```

```python
import functools

import jax
import jax.numpy as jnp
from jax import lax
from jax.experimental import pallas as pl
from jax.experimental.pallas import tpu as pltpu
from jax.sharding import PartitionSpec as P

CX = 4
CY = 32
NZ = 128
OUTER = 4
SWEEPS = 3
F32 = jnp.float32
BF16 = jnp.bfloat16
ROWS = CY + 8
PLANES = CX + 3
SPREAD = 288
QUANTITIES = 25
VMEM_BYTES = 48 * 1024 * 1024
ALL_VMEM_BYTES = 63 * 1024 * 1024


def in_vmem(count):
    return [pl.BlockSpec(memory_space=pltpu.VMEM)] * count


def in_smem():
    return pl.BlockSpec(memory_space=pltpu.SMEM)


def params(vmem_bytes=VMEM_BYTES):
    return pltpu.CompilerParams(vmem_limit_bytes=vmem_bytes)


def is_even():
    return lax.axis_index("gx") % 2 == 0


def across(n):
    return [(i, (i + 1) % n if i % 2 else (i - 1) % n) for i in range(n)]


def within(n):
    return [(i, i ^ 1) for i in range(n)]


def swap_x(to_within, to_across):
    n = lax.axis_size("gx")
    got_across = lax.ppermute(to_across, "gx", across(n))
    got_within = lax.ppermute(to_within, "gx", within(n))
    return got_within, got_across


def m4_weights(offset):
    remain = 1.0 - offset
    return (
        -0.5 * offset * remain * remain,
        1.0 - 2.5 * offset * offset + 1.5 * offset * offset * offset,
        1.0 - 2.5 * remain * remain + 1.5 * remain * remain * remain,
        -0.5 * offset * offset * remain,
    )


def prepare(cells, offsets, strengths, table, rows):
    weight_x, weight_y, weight_z = (m4_weights(offset) for offset in offsets)
    cell_x = cells // (CY * NZ)
    cell_y = cells // NZ % CY
    cell_z = cells % NZ
    for plane in range(PLANES):
        along = jnp.zeros_like(offsets[0])
        for tap in range(4):
            along = jnp.where(cell_x == plane - tap, weight_x[tap], along)
        table[plane, rows] = along
    table[11, rows] = (cell_y - 1).astype(F32)
    table[12, rows] = ((cell_z - 1) & (NZ - 1)).astype(F32)
    for tap in range(4):
        table[7 + tap, rows] = weight_y[tap]
        for comp in range(3):
            table[13 + tap * 3 + comp, rows] = weight_z[tap] * strengths[comp]


def spread(table, first, tiles, planes, lines):
    ids = lax.broadcasted_iota(jnp.int32, (8, 128), 0)
    zero = jnp.zeros((8, 128), F32)
    half = lax.broadcasted_iota(jnp.int32, (16, 128), 0) // 8
    none = jnp.zeros((16, 128), BF16)
    for tile in range(tiles):
        lanes = slice(tile * 128, (tile + 1) * 128)

        def figure(k):
            return table[k, pl.ds(first + tile, 1)]

        first_row = figure(11).astype(jnp.int32)
        tap_of = (ids - first_row) & 7
        row = first_row + tap_of
        row_tile = jnp.where(row < 0, CY // 8, row >> 3)
        taps = zero
        for tap in range(4):
            taps = jnp.where(tap_of == tap, figure(7 + tap), taps)
        along_y = [jnp.where(row_tile == k, taps, 0.0) for k in range(ROWS // 8)]
        parts = [figure(plane) * piece for plane in range(PLANES) for piece in along_y]
        parts += [zero] * ((SPREAD - PLANES * ROWS) // 8)
        planes[:, lanes] = jnp.concatenate(parts, axis=0).astype(BF16)

        first_z = figure(12).astype(jnp.int32)
        tap_of = (ids - first_z) & 7
        z_tile = (((first_z + tap_of) & (NZ - 1)) >> 3).astype(F32)
        where_tap = [tap_of == tap for tap in range(4)]
        pair = (jnp.concatenate([z_tile, z_tile], axis=0) - half.astype(F32)).astype(BF16)
        doubled = []
        for comp in range(3):
            taps = zero
            for tap in range(4):
                taps = jnp.where(where_tap[tap], figure(13 + tap * 3 + comp), taps)
            doubled.append(jnp.concatenate([taps, taps], axis=0).astype(BF16))
        for k in range(NZ // 16):
            here = pair == jnp.asarray(2.0 * k, BF16)
            for comp in range(3):
                start = comp * NZ + 16 * k
                lines[start : start + 16, lanes] = jnp.where(here, doubled[comp], none)


def product(planes, lines):
    return lax.dot_general(
        planes[...], lines[...], (((1,), (1,)), ((), ())), preferred_element_type=F32
    )


def leaving_kernel(
    moving, cell_hbm, offset_hbm, vort_hbm, to_within, to_across, cells, offsets, vorts, packed, sems, *, capacity
):
    room = 2 * capacity
    copies = [
        pltpu.make_async_copy(offset_hbm.at[:, pl.ds(0, room)], offsets, sems.at[0]),
        pltpu.make_async_copy(vort_hbm.at[:, pl.ds(0, room)], vorts, sems.at[1]),
        pltpu.make_async_copy(cell_hbm.at[pl.ds(0, room // 128)], cells, sems.at[2]),
    ]
    for copy in copies:
        copy.start()
    even = is_even()
    prev_count = moving[0, 0]
    next_count = moving[0, 1]
    for copy in copies:
        copy.wait()
    packed[0:3] = offsets[...]
    packed[3:6] = vorts[...]
    for tile in range(room // 128):
        packed[6:7, tile * 128 : (tile + 1) * 128] = cells[tile : tile + 1].astype(F32)
    packed[7:8] = jnp.zeros((1, room), F32)
    ids = lax.broadcasted_iota(jnp.int32, (8, capacity), 1)
    listed = packed[...]
    shifted = pltpu.roll(listed, (room - prev_count) % room, 1)
    for_prev = jnp.where(ids < prev_count, listed[:, :capacity], 0.0)
    for_next = jnp.where(ids < next_count, shifted[:, :capacity], 0.0)
    to_within[...] = jnp.where(even, for_next, for_prev)
    to_across[...] = jnp.where(even, for_prev, for_next)


def particle_specs():
    return [in_smem()] + [pl.BlockSpec(memory_space=pl.ANY)] * 3


def pack_leaving(moving, cells, part_offset, part_vort):
    slots = part_offset.shape[1]
    capacity = slots // 17
    room = 2 * capacity
    message = jax.ShapeDtypeStruct((8, capacity), F32)
    return pl.pallas_call(
        functools.partial(leaving_kernel, capacity=capacity),
        in_specs=particle_specs(),
        out_specs=tuple(in_vmem(2)),
        out_shape=(message, message),
        scratch_shapes=[
            pltpu.VMEM((room // 128, 128), jnp.int32),
            pltpu.VMEM((3, room), F32),
            pltpu.VMEM((3, room), F32),
            pltpu.VMEM((8, room), F32),
            pltpu.SemaphoreType.DMA((3,)),
        ],
        compiler_params=params(ALL_VMEM_BYTES),
    )(moving, cells, part_offset, part_vort)


def staying_kernel(
    moving, cells, offsets, vorts, total, dense, table, planes_a, lines_a, planes_b, lines_b, *, tiles_per_chunk
):
    first_stay = moving[0, 0] + moving[0, 1]
    live_len = moving[0, 2]
    tiles = cells.shape[0]
    total[...] = jnp.zeros_like(total)
    for tile in range(tiles):
        lanes = slice(tile * 128, (tile + 1) * 128)
        for dim in range(3):
            dense[dim, tile : tile + 1] = offsets[dim : dim + 1, lanes]
            dense[3 + dim, tile : tile + 1] = vorts[dim : dim + 1, lanes]

    def one_group(group, carry):
        rows = pl.ds(pl.multiple_of(group * 8, 8), 8)
        slot = (
            group * 1024
            + lax.broadcasted_iota(jnp.int32, (8, 128), 0) * 128
            + lax.broadcasted_iota(jnp.int32, (8, 128), 1)
        )
        keep = (slot >= first_stay) & (slot < live_len)
        prepare(
            cells[rows],
            [dense[dim, rows] for dim in range(3)],
            [jnp.where(keep, dense[3 + dim, rows], 0.0) for dim in range(3)],
            table,
            rows,
        )
        return carry

    lax.fori_loop(0, tiles // 8, one_group, 0)
    chunks = tiles // tiles_per_chunk
    spread(table, 0, tiles_per_chunk, planes_a, lines_a)

    def two_chunks(pair, carry):
        spread(table, (2 * pair + 1) * tiles_per_chunk, tiles_per_chunk, planes_b, lines_b)
        total[...] += product(planes_a, lines_a)
        spread(table, (2 * pair + 2) * tiles_per_chunk, tiles_per_chunk, planes_a, lines_a)
        total[...] += product(planes_b, lines_b)
        return carry

    lax.fori_loop(0, (chunks - 1) // 2, two_chunks, 0)
    if chunks % 2 == 0:
        spread(table, (chunks - 1) * tiles_per_chunk, tiles_per_chunk, planes_b, lines_b)
        total[...] += product(planes_a, lines_a)
        total[...] += product(planes_b, lines_b)
    else:
        total[...] += product(planes_a, lines_a)


def deposit_staying(moving, cells, part_offset, part_vort):
    tiles = cells.shape[0]
    slots = tiles * 128
    per_chunk = 17
    chunk = per_chunk * 128
    return pl.pallas_call(
        functools.partial(staying_kernel, tiles_per_chunk=per_chunk),
        in_specs=[in_smem()] + in_vmem(3),
        out_specs=in_vmem(1)[0],
        out_shape=jax.ShapeDtypeStruct((SPREAD, 3 * NZ), F32),
        scratch_shapes=[
            pltpu.VMEM((6, tiles, 128), F32),
            pltpu.VMEM((QUANTITIES, tiles, 128), F32),
        ]
        + [pltpu.VMEM((SPREAD, chunk), BF16), pltpu.VMEM((3 * NZ, chunk), BF16)] * 2,
        compiler_params=params(),
        cost_estimate=pl.CostEstimate(
            flops=2 * SPREAD * 3 * NZ * slots, bytes_accessed=28 * slots, transcendentals=0
        ),
    )(moving, cells, part_offset, part_vort)


def arrived_kernel(total, got_within, got_across, deposits, to_within, to_across, dense, table, planes, lines):
    tiles = got_within.shape[1] // 128
    for which, got in enumerate((got_within, got_across)):
        for tile in range(tiles):
            lanes = slice(tile * 128, (tile + 1) * 128)
            place = which * tiles + tile
            for k in range(7):
                dense[k, place : place + 1] = got[k : k + 1, lanes]
    for group in range(2 * tiles // 8):
        rows = slice(group * 8, (group + 1) * 8)
        prepare(
            dense[6, rows].astype(jnp.int32),
            [dense[dim, rows] for dim in range(3)],
            [dense[3 + dim, rows] for dim in range(3)],
            table,
            rows,
        )
    spread(table, 0, 2 * tiles, planes, lines)
    whole = total[...] + product(planes, lines)
    for comp in range(3):
        for plane in range(PLANES):
            deposits[comp, plane] = whole[
                plane * ROWS : (plane + 1) * ROWS, comp * NZ : (comp + 1) * NZ
            ]
    even = is_even()
    first_within = jnp.where(even, CX, 0)
    first_across = jnp.where(even, 0, CX)
    to_within[...] = deposits[:, pl.ds(first_within, 3)]
    to_across[...] = deposits[:, pl.ds(first_across, 3)]


def deposit_arrived(total, got_within, got_across):
    received = got_within.shape[1]
    edge = jax.ShapeDtypeStruct((3, 3, ROWS, NZ), F32)
    tiles = 2 * received // 128
    return pl.pallas_call(
        arrived_kernel,
        in_specs=in_vmem(3),
        out_specs=tuple(in_vmem(3)),
        out_shape=(jax.ShapeDtypeStruct((3, PLANES, ROWS, NZ), F32), edge, edge),
        scratch_shapes=[
            pltpu.VMEM((7, tiles, 128), F32),
            pltpu.VMEM((QUANTITIES, tiles, 128), F32),
            pltpu.VMEM((SPREAD, 2 * received), BF16),
            pltpu.VMEM((3 * NZ, 2 * received), BF16),
        ],
        compiler_params=params(),
    )(total, got_within, got_across)


def edge_rows(low, high):
    ids = lax.broadcasted_iota(jnp.int32, (8, NZ), 0)
    return jnp.where(ids < 4, low, high)


def edged_plane(mine, other, ends_only=False):
    edges = edge_rows(other[:8], other[-8:])
    if ends_only:
        return jnp.concatenate([mine[-8:], edges, mine[:8]], axis=0)
    return jnp.concatenate([mine, edges], axis=0)


def roll_rows(value, shift):
    return pltpu.roll(value, shift % value.shape[0], 0)


def roll_z(value, shift):
    return pltpu.roll(value, shift % NZ, 1)


def relax(fields, sources):
    rows = sources[0].shape[0]
    first_edge = CY if rows == ROWS else 8
    ids = lax.broadcasted_iota(jnp.int32, (rows, NZ), 0)
    frozen = (ids > first_edge) & (ids < first_edge + 7)
    sweeps = SWEEPS
    if fields is None:
        none = jnp.zeros((rows, NZ), F32)
        inner = [jnp.where(frozen, 0.0, source * (1.0 / 6.0)) for source in sources]
        fields = [none] + inner + [none]
        sweeps = SWEEPS - 1
    for sweep in range(sweeps):
        fresh = list(fields)
        last = sweep == sweeps - 1
        for x in range(2 if last else 1, CX + (2 if last else 3)):
            centre = fields[x]
            summed = fields[x - 1] + fields[x + 1] + roll_rows(centre, 1) + roll_rows(centre, -1)
            summed = summed + roll_z(centre, 1) + roll_z(centre, -1) + sources[x - 1]
            fresh[x] = jnp.where(frozen, centre, summed * (1.0 / 6.0))
        fields = fresh
    return fields[2 : CX + 2]


def pack_rows(value, rows):
    ids = lax.broadcasted_iota(jnp.int32, (8, NZ), 0)
    a, b = value[:CY], value[CY:]
    first, last = b[:8], b[-8:]
    if rows == CY + 8:
        return jnp.concatenate([a, jnp.where(ids < 4, first, last)], axis=0)
    if rows == CY + 16:
        return jnp.concatenate([a, first, last], axis=0)
    middle = jnp.where(ids < 4, b[8:16], b[CY - 16 : CY - 8])
    return jnp.concatenate([a, first, middle, last], axis=0)


def unpack_rows(packed):
    a, b = packed[:CY], packed[CY:]
    if b.shape[0] == 24:
        b = jnp.concatenate([b[:16], b[8:]], axis=0)
    return a, b


def hand_out(potential, to_within, to_across):
    even = is_even()
    rows = to_within.shape[2]
    for comp in range(3):
        for x in range(2):
            low, high = (pack_rows(potential[comp, at], rows) for at in (x, CX - 2 + x))
            to_within[comp, x] = jnp.where(even, high, low)
            to_across[comp, x] = jnp.where(even, low, high)


def fold_kernel(deposits, got_within, got_across, mine, message):
    even = is_even()
    ids = lax.broadcasted_iota(jnp.int32, (8, NZ), 0)
    for comp in range(3):
        for x in range(CX + 2):
            value = deposits[comp, x]
            if x < 3:
                value = value + jnp.where(even, got_across[comp, x], got_within[comp, x])
            if x >= CX:
                value = value + jnp.where(even, got_within[comp, x - CX], got_across[comp, x - CX])
            mine[comp, x] = value
            edges = value[CY:]
            third = jnp.where(ids < 2, edges, jnp.where(ids == 2, roll_rows(edges, 3), value[16:24]))
            message[comp, x] = jnp.concatenate([value[:16], third, value[24:CY]], axis=0)


def first_kernel(mine, other, omega, potential, to_within, to_across):
    ids = lax.broadcasted_iota(jnp.int32, (8, NZ), 0)

    def folded(main, edges):
        low = main[:8] + jnp.where(ids < 2, edges, 0.0)
        high = main[CY - 8 : CY] + jnp.where(ids == 7, edges, 0.0)
        return jnp.concatenate([low, main[8 : CY - 8], high], axis=0)

    for comp in range(3):
        sources = ([], [])
        for x in range(CX + 2):
            a = mine[comp, x]
            b = other[comp, x]
            third = b[16:24]
            b_edges = jnp.where(ids < 2, third, roll_rows(third, 5))
            omega_a = folded(a[:CY], b_edges)
            omega_b = folded(b, a[CY:])
            omega[comp, x, :CY] = omega_a
            omega[comp, x, CY:] = omega_b
            sources[0].append(edged_plane(omega_a, omega_b))
            sources[1].append(edged_plane(omega_b, omega_a))
        for block in range(2):
            fields = relax(None, sources[block])
            for x in range(CX):
                potential[comp, x, block * CY : (block + 1) * CY] = fields[x][:CY]
    hand_out(potential, to_within, to_across)


def gathered(potential, got_within, got_across, comp):
    even = is_even()

    def chosen(pick, x):
        return unpack_rows(jnp.where(pick, got_within[comp, x], got_across[comp, x]))

    below = [chosen(jnp.logical_not(even), x) for x in range(2)]
    above = [chosen(even, x) for x in range(2)]
    middle = [unpack_rows(potential[comp, x]) for x in range(CX)]
    return below + middle + above


def next_kernel(omega, before, got_within, got_across, potential, to_within, to_across):
    ends_only = before.shape[2] == CY + 16
    for comp in range(3):
        pairs = gathered(before, got_within, got_across, comp)
        charge = [(omega[comp, x, :CY], omega[comp, x, CY:]) for x in range(CX + 2)]
        fields = relax([edged_plane(a, b) for a, b in pairs], [edged_plane(a, b) for a, b in charge])
        for x in range(CX):
            potential[comp, x, :CY] = fields[x][:CY]
        fields = relax(
            [edged_plane(b, a, ends_only) for a, b in pairs],
            [edged_plane(b, a, ends_only) for a, b in charge],
        )
        first = 16 if ends_only else 0
        last = 0 if ends_only else CY - 8
        for x in range(CX):
            potential[comp, x, CY : CY + 8] = fields[x][first : first + 8]
            potential[comp, x, CY + 8 :] = fields[x][last : last + 8]
    hand_out(potential, to_within, to_across)


def last_kernel(omega, potential, got_within, got_across, velocity, stretching):
    psi = []
    for comp in range(3):
        pairs = gathered(potential, got_within, got_across, comp)
        psi.append([edged_plane(a, b) for a, b in pairs])

    def slope_x(planes, x):
        return (planes[x + 1] - planes[x - 1]) * 0.5

    def slope_y(plane):
        return (roll_rows(plane, -1) - roll_rows(plane, 1)) * 0.5

    def slope_z(plane):
        return (roll_z(plane, -1) - roll_z(plane, 1)) * 0.5

    speeds = ([None], [None], [None])
    for x in range(1, CX + 3):
        speeds[0].append(slope_y(psi[2][x]) - slope_z(psi[1][x]))
        speeds[1].append(slope_z(psi[0][x]) - slope_x(psi[2], x))
        speeds[2].append(slope_x(psi[1], x) - slope_y(psi[0][x]))
    for comp in range(3):
        for x in range(CX):
            centre = speeds[comp][x + 2]
            velocity[comp, x] = centre[:CY]
            stretching[comp, x] = (
                omega[0, x + 1, :CY] * slope_x(speeds[comp], x + 2)[:CY]
                + omega[1, x + 1, :CY] * slope_y(centre)[:CY]
                + omega[2, x + 1, :CY] * slope_z(centre)[:CY]
            )


def array(*shape):
    return jax.ShapeDtypeStruct(shape, F32)


def on_vmem(kernel, outs, *args):
    return pl.pallas_call(
        kernel,
        in_specs=in_vmem(len(args)),
        out_specs=tuple(in_vmem(len(outs))),
        out_shape=outs,
        compiler_params=params(),
    )(*args)


def two_block_solve(deposits, to_within, to_across):
    planes = CX + 2
    mine, message = on_vmem(
        fold_kernel,
        (array(3, planes, ROWS, NZ), array(3, planes, CY, NZ)),
        deposits,
        *swap_x(to_within, to_across),
    )
    other = lax.ppermute(message, "gy", [(0, 1), (1, 0)])
    whole, ends = array(3, CX, 2 * CY, NZ), array(3, CX, CY + 16, NZ)
    depths = [CY + 24, CY + 16, CY + 16, CY + 8]
    edge = array(3, 2, depths[0], NZ)
    omega, potential, to_within, to_across = on_vmem(
        first_kernel, (array(3, planes, 2 * CY, NZ), whole, edge, edge), mine, other
    )
    for depth in depths[1:]:
        edge = array(3, 2, depth, NZ)
        potential, to_within, to_across = on_vmem(
            next_kernel, (ends, edge, edge), omega, potential, *swap_x(to_within, to_across)
        )
    block = array(3, CX, CY, NZ)
    return on_vmem(
        last_kernel, (block, block), omega, potential, *swap_x(to_within, to_across)
    )


def padded(value, sides, width):
    for axis, dim in sides:
        devices, length = (lax.axis_size(axis), value.shape[dim])
        up = [(i, (i + 1) % devices) for i in range(devices)]
        down = [(j, i) for i, j in up]
        last = lax.slice_in_dim(value, length - width, length, axis=dim)
        leading = lax.slice_in_dim(value, 0, width, axis=dim)
        before = lax.ppermute(last, axis, up)
        after = lax.ppermute(leading, axis, down)
        value = jnp.concatenate([before, value, after], axis=dim)
    return value


def jacobi_sweep(field, source):
    centre = field[..., 1:-1, 1:-1, :]
    summed = (
        field[..., :-2, 1:-1, :]
        + field[..., 2:, 1:-1, :]
        + field[..., 1:-1, :-2, :]
        + field[..., 1:-1, 2:, :]
    )
    summed = summed + jnp.roll(centre, 1, -1) + jnp.roll(centre, -1, -1) + source
    return field.at[..., 1:-1, 1:-1, :].set(summed / 6.0)


def slope_x(field):
    return (field[2:, 1:-1] - field[:-2, 1:-1]) * 0.5


def slope_y(field):
    return (field[1:-1, 2:] - field[1:-1, :-2]) * 0.5


def slope_z(field):
    centre = field[1:-1, 1:-1]
    return (jnp.roll(centre, -1, -1) - jnp.roll(centre, 1, -1)) * 0.5


def fold_ghosts(extended, axis_dim, extent):
    centre = lax.slice_in_dim(extended, 4, extent + 4, axis=axis_dim)
    low_rim = lax.slice_in_dim(extended, 0, 2, axis=axis_dim)
    high_rim = lax.slice_in_dim(extended, extent + 6, extent + 8, axis=axis_dim)
    pad_low = [(0, 0)] * extended.ndim
    pad_high = [(0, 0)] * extended.ndim
    pad_low[axis_dim] = (0, extent - 2)
    pad_high[axis_dim] = (extent - 2, 0)
    return centre + jnp.pad(low_rim, pad_low) + jnp.pad(high_rim, pad_high)


def general_solve(deposits):
    sides = (("gx", 1), ("gy", 2))
    rows = jnp.concatenate(
        [jnp.zeros_like(deposits[:, :, :1]), deposits[:, :, ROWS - 1 :], deposits[:, :, : CY + 2]],
        axis=2,
    )
    full = jnp.pad(rows, ((0, 0), (1, 0), (0, 0), (0, 0)))
    omega = fold_ghosts(fold_ghosts(padded(full, sides, 2), 1, CX), 2, CY)
    source = padded(omega, sides, 2)[:, 1:-1, 1:-1]
    potential = jnp.zeros_like(omega)
    for _ in range(OUTER):
        field = padded(potential, sides, 2)
        for _ in range(SWEEPS):
            field = jacobi_sweep(field, source)
        potential = field[:, 2:-2, 2:-2]
    wide = padded(potential, sides, 2)
    edged_velocity = jnp.stack(
        [
            slope_y(wide[2]) - slope_z(wide[1]),
            slope_z(wide[0]) - slope_x(wide[2]),
            slope_x(wide[1]) - slope_y(wide[0]),
        ]
    )
    stretching = jnp.stack(
        [
            omega[0] * slope_x(edged_velocity[comp])
            + omega[1] * slope_y(edged_velocity[comp])
            + omega[2] * slope_z(edged_velocity[comp])
            for comp in range(3)
        ]
    )
    return edged_velocity[:, 1:-1, 1:-1], stretching


def per_device(part_cell, part_offset, part_vort, moving):
    particles = (moving, part_cell.reshape(-1, 128), part_offset, part_vort)
    got_within, got_across = swap_x(*pack_leaving(*particles))
    total = deposit_staying(*particles)
    deposits, to_within, to_across = deposit_arrived(total, got_within, got_across)
    if lax.axis_size("gy") == 2:
        return two_block_solve(deposits, to_within, to_across)
    return general_solve(deposits)


def solution(mesh):
    return jax.shard_map(
        per_device,
        mesh=mesh,
        in_specs=(
            P(("gx", "gy")),
            P(None, ("gx", "gy")),
            P(None, ("gx", "gy")),
            P(("gx", "gy"), None),
        ),
        out_specs=(P(None, "gx", "gy", None), P(None, "gx", "gy", None)),
        check_vma=False,
    )
```

```python
import functools

import jax
import jax.numpy as jnp
from jax import lax
from jax.experimental import pallas as pl
from jax.experimental.pallas import tpu as pltpu
from jax.sharding import PartitionSpec as P

CX = 4
CY = 32
NZ = 128
OUTER = 4
SWEEPS = 3
F32 = jnp.float32
BF16 = jnp.bfloat16
ROWS = CY + 8
PLANES = CX + 3
SPREAD = 288
QUANTITIES = 25
VMEM_BYTES = 48 * 1024 * 1024
ALL_VMEM_BYTES = 63 * 1024 * 1024


def in_vmem(count):
    return [pl.BlockSpec(memory_space=pltpu.VMEM)] * count


def in_smem():
    return pl.BlockSpec(memory_space=pltpu.SMEM)


def params(vmem_bytes=VMEM_BYTES):
    return pltpu.CompilerParams(vmem_limit_bytes=vmem_bytes)


def is_even():
    return lax.axis_index("gx") % 2 == 0


def across(n):
    return [(i, (i + 1) % n if i % 2 else (i - 1) % n) for i in range(n)]


def within(n):
    return [(i, i ^ 1) for i in range(n)]


def swap_x(to_within, to_across):
    n = lax.axis_size("gx")
    got_across = lax.ppermute(to_across, "gx", across(n))
    got_within = lax.ppermute(to_within, "gx", within(n))
    return got_across, got_within


def m4_weights(offset):
    remain = 1.0 - offset
    return (
        -0.5 * offset * remain * remain,
        1.0 - 2.5 * offset * offset + 1.5 * offset * offset * offset,
        1.0 - 2.5 * remain * remain + 1.5 * remain * remain * remain,
        -0.5 * offset * offset * remain,
    )


def prepare(cells, offsets, strengths, table, rows):
    weight_x, weight_y, weight_z = (m4_weights(offset) for offset in offsets)
    cell_x = cells // (CY * NZ)
    cell_y = cells // NZ % CY
    cell_z = cells % NZ
    for plane in range(PLANES):
        along = jnp.zeros_like(offsets[0])
        for tap in range(4):
            along = jnp.where(cell_x == plane - tap, weight_x[tap], along)
        table[plane, rows] = along
    table[11, rows] = (cell_y - 1).astype(F32)
    table[12, rows] = ((cell_z - 1) & (NZ - 1)).astype(F32)
    for tap in range(4):
        table[7 + tap, rows] = weight_y[tap]
        for comp in range(3):
            table[13 + tap * 3 + comp, rows] = weight_z[tap] * strengths[comp]


def spread(table, first, tiles, planes, lines):
    ids = lax.broadcasted_iota(jnp.int32, (8, 128), 0)
    zero = jnp.zeros((8, 128), F32)
    half = lax.broadcasted_iota(jnp.int32, (16, 128), 0) // 8
    none = jnp.zeros((16, 128), BF16)
    for tile in range(tiles):
        lanes = slice(tile * 128, (tile + 1) * 128)

        def figure(k):
            return table[k, pl.ds(first + tile, 1)]

        first_row = figure(11).astype(jnp.int32)
        tap_of = (ids - first_row) & 7
        row = first_row + tap_of
        row_tile = jnp.where(row < 0, CY // 8, row >> 3)
        taps = zero
        for tap in range(4):
            taps = jnp.where(tap_of == tap, figure(7 + tap), taps)
        along_y = [jnp.where(row_tile == k, taps, 0.0) for k in range(ROWS // 8)]
        parts = [figure(plane) * piece for plane in range(PLANES) for piece in along_y]
        parts += [zero] * ((SPREAD - PLANES * ROWS) // 8)
        planes[:, lanes] = jnp.concatenate(parts, axis=0).astype(BF16)

        first_z = figure(12).astype(jnp.int32)
        tap_of = (ids - first_z) & 7
        z_tile = (((first_z + tap_of) & (NZ - 1)) >> 3).astype(F32)
        where_tap = [tap_of == tap for tap in range(4)]
        pair = (jnp.concatenate([z_tile, z_tile], axis=0) - half.astype(F32)).astype(BF16)
        doubled = []
        for comp in range(3):
            taps = zero
            for tap in range(4):
                taps = jnp.where(where_tap[tap], figure(13 + tap * 3 + comp), taps)
            doubled.append(jnp.concatenate([taps, taps], axis=0).astype(BF16))
        for k in range(NZ // 16):
            here = pair == jnp.asarray(2.0 * k, BF16)
            for comp in range(3):
                start = comp * NZ + 16 * k
                lines[start : start + 16, lanes] = jnp.where(here, doubled[comp], none)


def product(planes, lines):
    return lax.dot_general(
        planes[...], lines[...], (((1,), (1,)), ((), ())), preferred_element_type=F32
    )


def leaving_kernel(
    moving, cell_hbm, offset_hbm, vort_hbm, to_within, to_across, cells, offsets, vorts, packed, sems, *, capacity
):
    room = 2 * capacity
    copies = [
        pltpu.make_async_copy(offset_hbm.at[:, pl.ds(0, room)], offsets, sems.at[0]),
        pltpu.make_async_copy(vort_hbm.at[:, pl.ds(0, room)], vorts, sems.at[1]),
        pltpu.make_async_copy(cell_hbm.at[pl.ds(0, room // 128)], cells, sems.at[2]),
    ]
    for copy in copies:
        copy.start()
    even = is_even()
    prev_count = moving[0, 0]
    next_count = moving[0, 1]
    for copy in copies:
        copy.wait()
    packed[0:3] = offsets[...]
    packed[3:6] = vorts[...]
    for tile in range(room // 128):
        packed[6:7, tile * 128 : (tile + 1) * 128] = cells[tile : tile + 1].astype(F32)
    packed[7:8] = jnp.zeros((1, room), F32)
    ids = lax.broadcasted_iota(jnp.int32, (8, capacity), 1)
    listed = packed[...]
    shifted = pltpu.roll(listed, (room - prev_count) % room, 1)
    for_prev = jnp.where(ids < prev_count, listed[:, :capacity], 0.0)
    for_next = jnp.where(ids < next_count, shifted[:, :capacity], 0.0)
    to_within[...] = jnp.where(even, for_next, for_prev)
    to_across[...] = jnp.where(even, for_prev, for_next)


def particle_specs():
    return [in_smem()] + [pl.BlockSpec(memory_space=pl.ANY)] * 3


def pack_leaving(moving, cells, part_offset, part_vort):
    slots = part_offset.shape[1]
    capacity = slots // 17
    room = 2 * capacity
    message = jax.ShapeDtypeStruct((8, capacity), F32)
    return pl.pallas_call(
        functools.partial(leaving_kernel, capacity=capacity),
        in_specs=particle_specs(),
        out_specs=tuple(in_vmem(2)),
        out_shape=(message, message),
        scratch_shapes=[
            pltpu.VMEM((room // 128, 128), jnp.int32),
            pltpu.VMEM((3, room), F32),
            pltpu.VMEM((3, room), F32),
            pltpu.VMEM((8, room), F32),
            pltpu.SemaphoreType.DMA((3,)),
        ],
        compiler_params=params(ALL_VMEM_BYTES),
    )(moving, cells, part_offset, part_vort)


def staying_kernel(
    moving, cells, offsets, vorts, total, dense, table, planes_a, lines_a, planes_b, lines_b, *, tiles_per_chunk
):
    first_stay = moving[0, 0] + moving[0, 1]
    live_len = moving[0, 2]
    tiles = cells.shape[0]
    total[...] = jnp.zeros_like(total)
    for tile in range(tiles):
        lanes = slice(tile * 128, (tile + 1) * 128)
        for dim in range(3):
            dense[dim, tile : tile + 1] = offsets[dim : dim + 1, lanes]
            dense[3 + dim, tile : tile + 1] = vorts[dim : dim + 1, lanes]

    def one_group(group, carry):
        rows = pl.ds(pl.multiple_of(group * 8, 8), 8)
        slot = (
            group * 1024
            + lax.broadcasted_iota(jnp.int32, (8, 128), 0) * 128
            + lax.broadcasted_iota(jnp.int32, (8, 128), 1)
        )
        keep = (slot >= first_stay) & (slot < live_len)
        prepare(
            cells[rows],
            [dense[dim, rows] for dim in range(3)],
            [jnp.where(keep, dense[3 + dim, rows], 0.0) for dim in range(3)],
            table,
            rows,
        )
        return carry

    lax.fori_loop(0, tiles // 8, one_group, 0)
    chunks = tiles // tiles_per_chunk
    spread(table, 0, tiles_per_chunk, planes_a, lines_a)

    def two_chunks(pair, carry):
        spread(table, (2 * pair + 1) * tiles_per_chunk, tiles_per_chunk, planes_b, lines_b)
        total[...] += product(planes_a, lines_a)
        spread(table, (2 * pair + 2) * tiles_per_chunk, tiles_per_chunk, planes_a, lines_a)
        total[...] += product(planes_b, lines_b)
        return carry

    lax.fori_loop(0, (chunks - 1) // 2, two_chunks, 0)
    if chunks % 2 == 0:
        spread(table, (chunks - 1) * tiles_per_chunk, tiles_per_chunk, planes_b, lines_b)
        total[...] += product(planes_a, lines_a)
        total[...] += product(planes_b, lines_b)
    else:
        total[...] += product(planes_a, lines_a)


def deposit_staying(moving, cells, part_offset, part_vort):
    tiles = cells.shape[0]
    slots = tiles * 128
    per_chunk = 17
    chunk = per_chunk * 128
    return pl.pallas_call(
        functools.partial(staying_kernel, tiles_per_chunk=per_chunk),
        in_specs=[in_smem()] + in_vmem(3),
        out_specs=in_vmem(1)[0],
        out_shape=jax.ShapeDtypeStruct((SPREAD, 3 * NZ), F32),
        scratch_shapes=[
            pltpu.VMEM((6, tiles, 128), F32),
            pltpu.VMEM((QUANTITIES, tiles, 128), F32),
        ]
        + [pltpu.VMEM((SPREAD, chunk), BF16), pltpu.VMEM((3 * NZ, chunk), BF16)] * 2,
        compiler_params=params(),
        cost_estimate=pl.CostEstimate(
            flops=2 * SPREAD * 3 * NZ * slots, bytes_accessed=28 * slots, transcendentals=0
        ),
    )(moving, cells, part_offset, part_vort)


def arrived_kernel(total, got_across, got_within, deposits, to_within, to_across, dense, table, planes, lines):
    tiles = got_within.shape[1] // 128
    for which, got in enumerate((got_across, got_within)):
        for tile in range(tiles):
            lanes = slice(tile * 128, (tile + 1) * 128)
            place = which * tiles + tile
            for k in range(7):
                dense[k, place : place + 1] = got[k : k + 1, lanes]
    for group in range(2 * tiles // 8):
        rows = slice(group * 8, (group + 1) * 8)
        prepare(
            dense[6, rows].astype(jnp.int32),
            [dense[dim, rows] for dim in range(3)],
            [dense[3 + dim, rows] for dim in range(3)],
            table,
            rows,
        )
    spread(table, 0, 2 * tiles, planes, lines)
    whole = total[...] + product(planes, lines)
    for comp in range(3):
        for plane in range(PLANES):
            deposits[comp, plane] = whole[
                plane * ROWS : (plane + 1) * ROWS, comp * NZ : (comp + 1) * NZ
            ]
    even = is_even()
    first_within = jnp.where(even, CX, 0)
    first_across = jnp.where(even, 0, CX)
    to_within[...] = deposits[:, pl.ds(first_within, 3)]
    to_across[...] = deposits[:, pl.ds(first_across, 3)]


def deposit_arrived(total, got_across, got_within):
    received = got_within.shape[1]
    edge = jax.ShapeDtypeStruct((3, 3, ROWS, NZ), F32)
    tiles = 2 * received // 128
    return pl.pallas_call(
        arrived_kernel,
        in_specs=in_vmem(3),
        out_specs=tuple(in_vmem(3)),
        out_shape=(jax.ShapeDtypeStruct((3, PLANES, ROWS, NZ), F32), edge, edge),
        scratch_shapes=[
            pltpu.VMEM((7, tiles, 128), F32),
            pltpu.VMEM((QUANTITIES, tiles, 128), F32),
            pltpu.VMEM((SPREAD, 2 * received), BF16),
            pltpu.VMEM((3 * NZ, 2 * received), BF16),
        ],
        compiler_params=params(),
    )(total, got_across, got_within)


def edge_rows(low, high):
    ids = lax.broadcasted_iota(jnp.int32, (8, NZ), 0)
    return jnp.where(ids < 4, low, high)


def edged_plane(mine, other, ends_only=False):
    edges = edge_rows(other[:8], other[-8:])
    if ends_only:
        return jnp.concatenate([mine[-8:], edges, mine[:8]], axis=0)
    return jnp.concatenate([mine, edges], axis=0)


def roll_rows(value, shift):
    return pltpu.roll(value, shift % value.shape[0], 0)


def roll_z(value, shift):
    return pltpu.roll(value, shift % NZ, 1)


def relax(fields, sources):
    rows = sources[0].shape[0]
    first_edge = CY if rows == ROWS else 8
    ids = lax.broadcasted_iota(jnp.int32, (rows, NZ), 0)
    frozen = (ids > first_edge) & (ids < first_edge + 7)
    sweeps = SWEEPS
    if fields is None:
        none = jnp.zeros((rows, NZ), F32)
        inner = [jnp.where(frozen, 0.0, source * (1.0 / 6.0)) for source in sources]
        fields = [none] + inner + [none]
        sweeps = SWEEPS - 1
    for sweep in range(sweeps):
        fresh = list(fields)
        last = sweep == sweeps - 1
        for x in range(2 if last else 1, CX + (2 if last else 3)):
            centre = fields[x]
            summed = fields[x - 1] + fields[x + 1] + roll_rows(centre, 1) + roll_rows(centre, -1)
            summed = summed + roll_z(centre, 1) + roll_z(centre, -1) + sources[x - 1]
            fresh[x] = jnp.where(frozen, centre, summed * (1.0 / 6.0))
        fields = fresh
    return fields[2 : CX + 2]


def pack_rows(value, rows):
    ids = lax.broadcasted_iota(jnp.int32, (8, NZ), 0)
    a, b = value[:CY], value[CY:]
    first, last = b[:8], b[-8:]
    if rows == CY + 8:
        return jnp.concatenate([a, jnp.where(ids < 4, first, last)], axis=0)
    if rows == CY + 16:
        return jnp.concatenate([a, first, last], axis=0)
    middle = jnp.where(ids < 4, b[8:16], b[CY - 16 : CY - 8])
    return jnp.concatenate([a, first, middle, last], axis=0)


def unpack_rows(packed):
    a, b = packed[:CY], packed[CY:]
    if b.shape[0] == 24:
        b = jnp.concatenate([b[:16], b[8:]], axis=0)
    return a, b


def hand_out(potential, to_within, to_across):
    even = is_even()
    rows = to_within.shape[2]
    for comp in range(3):
        for x in range(2):
            low, high = (pack_rows(potential[comp, at], rows) for at in (x, CX - 2 + x))
            to_within[comp, x] = jnp.where(even, high, low)
            to_across[comp, x] = jnp.where(even, low, high)


def fold_kernel(deposits, got_across, got_within, mine, message):
    even = is_even()
    ids = lax.broadcasted_iota(jnp.int32, (8, NZ), 0)
    for comp in range(3):
        for x in range(CX + 2):
            value = deposits[comp, x]
            if x < 3:
                value = value + jnp.where(even, got_across[comp, x], got_within[comp, x])
            if x >= CX:
                value = value + jnp.where(even, got_within[comp, x - CX], got_across[comp, x - CX])
            mine[comp, x] = value
            edges = value[CY:]
            third = jnp.where(ids < 2, edges, jnp.where(ids == 2, roll_rows(edges, 3), value[16:24]))
            message[comp, x] = jnp.concatenate([value[:16], third, value[24:CY]], axis=0)


def first_kernel(mine, other, omega, potential, to_within, to_across):
    ids = lax.broadcasted_iota(jnp.int32, (8, NZ), 0)

    def folded(main, edges):
        low = main[:8] + jnp.where(ids < 2, edges, 0.0)
        high = main[CY - 8 : CY] + jnp.where(ids == 7, edges, 0.0)
        return jnp.concatenate([low, main[8 : CY - 8], high], axis=0)

    for comp in range(3):
        sources = ([], [])
        for x in range(CX + 2):
            a = mine[comp, x]
            b = other[comp, x]
            third = b[16:24]
            b_edges = jnp.where(ids < 2, third, roll_rows(third, 5))
            omega_a = folded(a[:CY], b_edges)
            omega_b = folded(b, a[CY:])
            omega[comp, x, :CY] = omega_a
            omega[comp, x, CY:] = omega_b
            sources[0].append(edged_plane(omega_a, omega_b))
            sources[1].append(edged_plane(omega_b, omega_a))
        for block in range(2):
            fields = relax(None, sources[block])
            for x in range(CX):
                potential[comp, x, block * CY : (block + 1) * CY] = fields[x][:CY]
    hand_out(potential, to_within, to_across)


def gathered(potential, got_across, got_within, comp):
    even = is_even()

    def chosen(pick, x):
        return unpack_rows(jnp.where(pick, got_within[comp, x], got_across[comp, x]))

    below = [chosen(jnp.logical_not(even), x) for x in range(2)]
    above = [chosen(even, x) for x in range(2)]
    middle = [unpack_rows(potential[comp, x]) for x in range(CX)]
    return below + middle + above


def next_kernel(omega, before, got_across, got_within, potential, to_within, to_across):
    ends_only = before.shape[2] == CY + 16
    for comp in range(3):
        pairs = gathered(before, got_across, got_within, comp)
        charge = [(omega[comp, x, :CY], omega[comp, x, CY:]) for x in range(CX + 2)]
        fields = relax([edged_plane(a, b) for a, b in pairs], [edged_plane(a, b) for a, b in charge])
        for x in range(CX):
            potential[comp, x, :CY] = fields[x][:CY]
        fields = relax(
            [edged_plane(b, a, ends_only) for a, b in pairs],
            [edged_plane(b, a, ends_only) for a, b in charge],
        )
        first = 16 if ends_only else 0
        last = 0 if ends_only else CY - 8
        for x in range(CX):
            potential[comp, x, CY : CY + 8] = fields[x][first : first + 8]
            potential[comp, x, CY + 8 :] = fields[x][last : last + 8]
    hand_out(potential, to_within, to_across)


def last_kernel(omega, potential, got_across, got_within, velocity, stretching):
    psi = []
    for comp in range(3):
        pairs = gathered(potential, got_across, got_within, comp)
        psi.append([edged_plane(a, b) for a, b in pairs])

    def slope_x(planes, x):
        return (planes[x + 1] - planes[x - 1]) * 0.5

    def slope_y(plane):
        return (roll_rows(plane, -1) - roll_rows(plane, 1)) * 0.5

    def slope_z(plane):
        return (roll_z(plane, -1) - roll_z(plane, 1)) * 0.5

    speeds = ([None], [None], [None])
    for x in range(1, CX + 3):
        speeds[0].append(slope_y(psi[2][x]) - slope_z(psi[1][x]))
        speeds[1].append(slope_z(psi[0][x]) - slope_x(psi[2], x))
        speeds[2].append(slope_x(psi[1], x) - slope_y(psi[0][x]))
    for comp in range(3):
        for x in range(CX):
            centre = speeds[comp][x + 2]
            velocity[comp, x] = centre[:CY]
            stretching[comp, x] = (
                omega[0, x + 1, :CY] * slope_x(speeds[comp], x + 2)[:CY]
                + omega[1, x + 1, :CY] * slope_y(centre)[:CY]
                + omega[2, x + 1, :CY] * slope_z(centre)[:CY]
            )


def array(*shape):
    return jax.ShapeDtypeStruct(shape, F32)


def on_vmem(kernel, outs, *args):
    return pl.pallas_call(
        kernel,
        in_specs=in_vmem(len(args)),
        out_specs=tuple(in_vmem(len(outs))),
        out_shape=outs,
        compiler_params=params(),
    )(*args)


def two_block_solve(deposits, to_within, to_across):
    planes = CX + 2
    mine, message = on_vmem(
        fold_kernel,
        (array(3, planes, ROWS, NZ), array(3, planes, CY, NZ)),
        deposits,
        *swap_x(to_within, to_across),
    )
    other = lax.ppermute(message, "gy", [(0, 1), (1, 0)])
    whole, ends = array(3, CX, 2 * CY, NZ), array(3, CX, CY + 16, NZ)
    depths = [CY + 24, CY + 16, CY + 16, CY + 8]
    edge = array(3, 2, depths[0], NZ)
    omega, potential, to_within, to_across = on_vmem(
        first_kernel, (array(3, planes, 2 * CY, NZ), whole, edge, edge), mine, other
    )
    for depth in depths[1:]:
        edge = array(3, 2, depth, NZ)
        potential, to_within, to_across = on_vmem(
            next_kernel, (ends, edge, edge), omega, potential, *swap_x(to_within, to_across)
        )
    block = array(3, CX, CY, NZ)
    return on_vmem(
        last_kernel, (block, block), omega, potential, *swap_x(to_within, to_across)
    )


def padded(value, sides, width):
    for axis, dim in sides:
        devices, length = (lax.axis_size(axis), value.shape[dim])
        up = [(i, (i + 1) % devices) for i in range(devices)]
        down = [(j, i) for i, j in up]
        last = lax.slice_in_dim(value, length - width, length, axis=dim)
        leading = lax.slice_in_dim(value, 0, width, axis=dim)
        before = lax.ppermute(last, axis, up)
        after = lax.ppermute(leading, axis, down)
        value = jnp.concatenate([before, value, after], axis=dim)
    return value


def jacobi_sweep(field, source):
    centre = field[..., 1:-1, 1:-1, :]
    summed = (
        field[..., :-2, 1:-1, :]
        + field[..., 2:, 1:-1, :]
        + field[..., 1:-1, :-2, :]
        + field[..., 1:-1, 2:, :]
    )
    summed = summed + jnp.roll(centre, 1, -1) + jnp.roll(centre, -1, -1) + source
    return field.at[..., 1:-1, 1:-1, :].set(summed / 6.0)


def slope_x(field):
    return (field[2:, 1:-1] - field[:-2, 1:-1]) * 0.5


def slope_y(field):
    return (field[1:-1, 2:] - field[1:-1, :-2]) * 0.5


def slope_z(field):
    centre = field[1:-1, 1:-1]
    return (jnp.roll(centre, -1, -1) - jnp.roll(centre, 1, -1)) * 0.5


def fold_ghosts(extended, axis_dim, extent):
    centre = lax.slice_in_dim(extended, 4, extent + 4, axis=axis_dim)
    low_rim = lax.slice_in_dim(extended, 0, 2, axis=axis_dim)
    high_rim = lax.slice_in_dim(extended, extent + 6, extent + 8, axis=axis_dim)
    pad_low = [(0, 0)] * extended.ndim
    pad_high = [(0, 0)] * extended.ndim
    pad_low[axis_dim] = (0, extent - 2)
    pad_high[axis_dim] = (extent - 2, 0)
    return centre + jnp.pad(low_rim, pad_low) + jnp.pad(high_rim, pad_high)


def general_solve(deposits):
    sides = (("gx", 1), ("gy", 2))
    rows = jnp.concatenate(
        [jnp.zeros_like(deposits[:, :, :1]), deposits[:, :, ROWS - 1 :], deposits[:, :, : CY + 2]],
        axis=2,
    )
    full = jnp.pad(rows, ((0, 0), (1, 0), (0, 0), (0, 0)))
    omega = fold_ghosts(fold_ghosts(padded(full, sides, 2), 1, CX), 2, CY)
    source = padded(omega, sides, 2)[:, 1:-1, 1:-1]
    potential = jnp.zeros_like(omega)
    for _ in range(OUTER):
        field = padded(potential, sides, 2)
        for _ in range(SWEEPS):
            field = jacobi_sweep(field, source)
        potential = field[:, 2:-2, 2:-2]
    wide = padded(potential, sides, 2)
    edged_velocity = jnp.stack(
        [
            slope_y(wide[2]) - slope_z(wide[1]),
            slope_z(wide[0]) - slope_x(wide[2]),
            slope_x(wide[1]) - slope_y(wide[0]),
        ]
    )
    stretching = jnp.stack(
        [
            omega[0] * slope_x(edged_velocity[comp])
            + omega[1] * slope_y(edged_velocity[comp])
            + omega[2] * slope_z(edged_velocity[comp])
            for comp in range(3)
        ]
    )
    return edged_velocity[:, 1:-1, 1:-1], stretching


def per_device(part_cell, part_offset, part_vort, moving):
    particles = (moving, part_cell.reshape(-1, 128), part_offset, part_vort)
    got_across, got_within = swap_x(*pack_leaving(*particles))
    total = deposit_staying(*particles)
    deposits, to_within, to_across = deposit_arrived(total, got_across, got_within)
    if lax.axis_size("gy") == 2:
        return two_block_solve(deposits, to_within, to_across)
    return general_solve(deposits)


def solution(mesh):
    return jax.shard_map(
        per_device,
        mesh=mesh,
        in_specs=(
            P(("gx", "gy")),
            P(None, ("gx", "gy")),
            P(None, ("gx", "gy")),
            P(("gx", "gy"), None),
        ),
        out_specs=(P(None, "gx", "gy", None), P(None, "gx", "gy", None)),
        check_vma=False,
    )
```
